256 devices in a mesh: tp: 4 (over x), ep: 64 (over z, y, core).
Axes of the slice: x: 4, y: 4, z: 8, core: 2. Of those that a mesh axis runs over, the one named last changes fastest.
Arguments:
- tokens: bfloat16 [32768, 2048], P(('tp', 'ep')), may hold values from -6 to 6
- expert_ids: int32 [32768, 2], P(('tp', 'ep')), may hold values from 0 to 255, all different within a row; in each aligned block of 128 rows (0 to 127, 128 to 255, ...) at most 2 rows name the same one
- gate_weights: float32 [32768, 2], P(('tp', 'ep')), may hold values from 0.1 to 1
- grad_out: bfloat16 [32768, 2048], P(('tp', 'ep')), may hold values from -6 to 6
- expert_gate: bfloat16 [256, 2048, 512], P(('tp', 'ep')), may hold values from -0.125 to 0.125
- expert_up: bfloat16 [256, 2048, 512], P(('tp', 'ep')), may hold values from -0.125 to 0.125
- expert_down: bfloat16 [256, 512, 2048], P(('tp', 'ep')), may hold values from -0.25 to 0.25
- shared_gate: bfloat16 [2048, 512], P(None, 'tp'), may hold values from -0.125 to 0.125
- shared_up: bfloat16 [2048, 512], P(None, 'tp'), may hold values from -0.125 to 0.125
- shared_down: bfloat16 [512, 2048], P('tp'), may hold values from -0.25 to 0.25
- shared_switch: bfloat16 [2048], replicated, may hold values from -0.29882812 to 0.29882812
Outputs:
- mixed: bfloat16 [32768, 2048], P(('tp', 'ep'))
- grad_tokens: bfloat16 [32768, 2048], P(('tp', 'ep'))
- gate_grad: float32 [32768, 2], P(('tp', 'ep'))
The draws below stay inside these ranges and needn't reach their ends.
Inputs may be any that keep to these rules, and one draw needn't show every extreme that they name: `expert_ids`: each row names 2 different experts; among the rows of one device no expert is named more than 2 times, a bound that some block reaches.
All inputs are finite; a program needn't handle non-finite values.
Results may differ from the reference program's by a relative error of at most 0.019.
Values may be sent and summed in bfloat16 or wider, within the bound.
No kernel may reach another device: no remote copies, remote signals or barrier semaphores. Data moves between devices by JAX's collectives and lax.ppermute only.
A program may use at most 128 MiB of HBM per device.

```python
import math
import jax
import jax.numpy as jnp
import numpy as np
from jax import lax

D = 2048
FF = 512
SFF = 512
TOK_DEV = 128
TOPK = 2
EXPERTS = 256
CAP = 2
TOKENS = 32768


def steps_of(own_key, dims, shards, smallest, top_value):
    level, own = 1.0, jax.random.fold_in(own_key, 6)
    for axis_at, parts in shards:
        heights = jnp.exp(jax.random.uniform(jax.random.fold_in(own, axis_at), (parts,), jnp.float32, smallest / len(shards), top_value / len(shards)))
        level = level * jnp.repeat(heights, dims[axis_at] // parts).reshape([-1 if axis == axis_at else 1 for axis in range(len(dims))])
    return level


def deal_out(own_key, own, number, rows, amount, top, most, skew):
    sequence = jax.random.permutation(own_key, amount)
    heavy_load, common = portions_of(amount, rows * top, most, skew, True), portions_of(amount, rows * top, most, skew, False)
    places = jnp.arange(amount)

    def named(sizes, offset_by):
        used = int((sizes > 0).sum())
        fixed = max(1, used // 4)
        shifted = fixed + (places - fixed + offset_by * (used - fixed)) % max(1, amount - fixed)
        return jnp.zeros((amount,), jnp.int32).at[sequence[jnp.where(places < fixed, places, shifted)]].set(jnp.asarray(sizes, jnp.int32))

    sizes = jnp.where(number % 4 == 0, named(heavy_load, number // 4), named(common, number - number // 4 - 1))
    mixed = jax.random.permutation(jax.random.fold_in(own, 3), amount)
    donor, receiver = mixed[0:amount // 2 * 2:2], mixed[1:amount // 2 * 2:2]
    margin = jnp.minimum(sizes[donor] - 1, most - sizes[receiver]) // 2
    margin = jnp.where((donor == sequence[0]) | (receiver == sequence[0]) | (sizes[receiver] == 0), 0, jnp.maximum(margin, 0))
    shifted = jax.random.randint(jax.random.fold_in(own, 4), (amount // 2,), 0, 1 << 20) % (margin + 1)
    sizes = sizes.at[donor].add(-shifted).at[receiver].add(shifted)
    items = jnp.searchsorted(jnp.cumsum(sizes), jnp.arange(rows * top), side="right").astype(jnp.int32)
    grid = items.reshape(top, rows).T
    grid = grid[jax.random.permutation(jax.random.fold_in(own, 1), rows)]
    offset_by = jax.random.randint(jax.random.fold_in(own, 2), (rows, 1), 0, top)
    return jnp.take_along_axis(grid, (jnp.arange(top)[None, :] + offset_by) % top, axis=1)


def portions_of(amount, total, most, lean, full):
    loads = [(1 << 20) // math.isqrt(standing ** lean) + 1 for standing in range(1, amount + 1)]
    largest = most if full else min(most, max(-(-total // amount), total * loads[0] // sum(loads)))
    least = 1 if total - largest >= amount - 1 else 0
    counts, surplus = [largest] + [least] * (amount - 1), total - largest - least * (amount - 1)
    while surplus > 0:
        free = [i for i in range(1, amount) if counts[i] < largest] or [i for i in range(1, amount) if counts[i] < most]
        whole, left = sum([loads[i] for i in free]), surplus
        for i in free:
            extra = min(most - counts[i], max(1, left * loads[i] // whole), surplus)
            counts[i] = counts[i] + extra
            surplus = surplus - extra
    return np.array(counts)


def bell_draw(stream_key, extent, scale, reach, pieces=(), kind=jnp.bfloat16):
    level = steps_of(stream_key, extent, pieces, -0.22, 0.18) if pieces else 1.0
    values = jax.random.normal(stream_key, extent, jnp.float32) * scale * level
    return jnp.minimum(jnp.maximum(values, -reach), reach).astype(kind)


def setup_inputs(seed: int = 0) -> dict:
    streams_of = jax.random.split(jax.random.key(seed), 12)
    tokens = bell_draw(streams_of[0], (TOKENS, D), 1.0, 6.0, ((0, 256),))
    expert_ids_keys = jax.random.split(jax.random.fold_in(streams_of[1], 1), TOKENS // TOK_DEV)
    expert_ids_turns = jax.random.permutation(jax.random.fold_in(streams_of[1], 3), TOKENS // TOK_DEV)
    expert_ids = jax.vmap(lambda own, number: deal_out(jax.random.fold_in(streams_of[1], 2), own, number, TOK_DEV, EXPERTS, TOPK, CAP, 1))(expert_ids_keys, expert_ids_turns).reshape((TOKENS, TOPK))
    gate_weights = jnp.clip(0.1 + 0.9 * jax.random.uniform(streams_of[2], (TOKENS, TOPK), jnp.float32) ** steps_of(streams_of[2], (TOKENS, TOPK), ((0, 256),), -0.2, 0.2), 0.1, 1.0)
    grad_out = bell_draw(streams_of[3], (TOKENS, D), 1.0, 6.0, ((0, 256),))
    expert_gate = bell_draw(streams_of[4], (EXPERTS, D, FF), D ** -0.5, 0.125, ((0, 256),))
    expert_up = bell_draw(streams_of[5], (EXPERTS, D, FF), D ** -0.5, 0.125, ((0, 256),))
    expert_down = bell_draw(streams_of[6], (EXPERTS, FF, D), FF ** -0.5, 0.25, ((0, 256),))
    shared_gate = bell_draw(streams_of[7], (D, SFF), D ** -0.5, 0.125, ((1, 4),))
    shared_up = bell_draw(streams_of[8], (D, SFF), D ** -0.5, 0.125, ((1, 4),))
    shared_down = bell_draw(streams_of[9], (SFF, D), SFF ** -0.5, 0.25, ((0, 4),))
    shared_switch = bell_draw(streams_of[10], (D,), 0.05, 0.29882812)
    return {"tokens": tokens, "expert_ids": expert_ids, "gate_weights": gate_weights, "grad_out": grad_out, "expert_gate": expert_gate, "expert_up": expert_up, "expert_down": expert_down, "shared_gate": shared_gate, "shared_up": shared_up, "shared_down": shared_down, "shared_switch": shared_switch}


def silu_grad(argument):
    gate_sig = jax.nn.sigmoid(argument)
    return gate_sig * (1.0 + argument * (1.0 - gate_sig))

def slot_sources(expert_ids):
    blocks = TOKENS // TOK_DEV
    pair_count = TOK_DEV * TOPK
    chosen = expert_ids.reshape(blocks, pair_count).astype(jnp.int32)
    onehot = (chosen[:, :, None] == jnp.arange(EXPERTS, dtype=jnp.int32)[None, None, :]).astype(jnp.int32)
    before = jnp.cumsum(onehot, axis=1) - onehot
    position = lax.optimization_barrier(jnp.sum(before * onehot, axis=2)).astype(jnp.int32)
    slot_index = (chosen * CAP + position).astype(jnp.int32)
    pair_index = jnp.arange(blocks, dtype=jnp.int32)[:, None] * pair_count + jnp.arange(pair_count, dtype=jnp.int32)[None, :]
    block_index = jnp.broadcast_to(jnp.arange(blocks, dtype=jnp.int32)[:, None], (blocks, pair_count))
    source_table = jnp.full((blocks, EXPERTS * CAP), -1, jnp.int32)
    source_table = source_table.at[block_index, slot_index].set(pair_index.astype(jnp.int32))
    return source_table.reshape(blocks, EXPERTS, CAP).transpose(1, 0, 2).reshape(EXPERTS, blocks * CAP)

def reference(tokens, expert_ids, gate_weights, grad_out, expert_gate, expert_up, expert_down, shared_gate, shared_up, shared_down, shared_switch):
    source_table = slot_sources(expert_ids)
    flat_gates = gate_weights.reshape(-1)

    def per_expert(totals, inputs):
        mixed_sum, grad_sum, gate_sum = totals
        sources, w_gate, w_up, w_down = inputs
        is_live = sources >= 0
        pair_idx = jnp.where(is_live, sources, 0).astype(jnp.int32)
        token_row = (pair_idx // TOPK).astype(jnp.int32)
        weighting = jnp.where(is_live, flat_gates[pair_idx], jnp.zeros((), jnp.float32))
        picked = tokens[token_row]
        pre_gate = jnp.dot(picked, w_gate, preferred_element_type=jnp.float32)
        pre_up = jnp.dot(picked, w_up, preferred_element_type=jnp.float32)
        hidden = (jax.nn.silu(pre_gate) * pre_up).astype(jnp.bfloat16)
        output = jnp.dot(hidden, w_down, preferred_element_type=jnp.float32)
        routed = (weighting[:, None] * output).astype(jnp.bfloat16)
        cotangent = jnp.where(is_live[:, None], grad_out[token_row], jnp.zeros((), grad_out.dtype))
        slot_grad = lax.optimization_barrier(jnp.sum(cotangent.astype(jnp.float32) * output, axis=1))
        scaled = (weighting[:, None] * cotangent.astype(jnp.float32)).astype(jnp.bfloat16)
        hidden_grad = jnp.dot(scaled, w_down.T, preferred_element_type=jnp.float32)
        gate_part = (hidden_grad * pre_up * silu_grad(pre_gate)).astype(jnp.bfloat16)
        up_part = (hidden_grad * jax.nn.silu(pre_gate)).astype(jnp.bfloat16)
        input_grad = (jnp.dot(gate_part, w_gate.T, preferred_element_type=jnp.float32) + jnp.dot(up_part, w_up.T, preferred_element_type=jnp.float32)).astype(jnp.bfloat16)
        mixed_sum = mixed_sum.at[token_row].add(routed.astype(jnp.float32))
        grad_sum = grad_sum.at[token_row].add(input_grad.astype(jnp.float32))
        gate_sum = gate_sum.at[pair_idx].add(jnp.where(is_live, slot_grad, jnp.zeros((), jnp.float32)))
        return ((mixed_sum, grad_sum, gate_sum), None)
    start = (jnp.zeros((TOKENS, D), jnp.float32), jnp.zeros((TOKENS, D), jnp.float32), jnp.zeros((TOKENS * TOPK,), jnp.float32))
    totals, unused = lax.scan(per_expert, start, (source_table, expert_gate, expert_up, expert_down))
    mixed_sum, grad_sum, gate_sum = totals
    switch_logit = jnp.dot(tokens, shared_switch, preferred_element_type=jnp.float32)
    switch = jax.nn.sigmoid(switch_logit)
    shared_pre_gate = jnp.dot(tokens, shared_gate, preferred_element_type=jnp.float32)
    shared_pre_up = jnp.dot(tokens, shared_up, preferred_element_type=jnp.float32)
    shared_hidden = (jax.nn.silu(shared_pre_gate) * shared_pre_up).astype(jnp.bfloat16)
    shared = jnp.dot(shared_hidden, shared_down, preferred_element_type=jnp.float32)
    mixed = (switch[:, None] * shared + mixed_sum).astype(jnp.bfloat16)
    switch_grad = switch * (1.0 - switch) * lax.optimization_barrier(jnp.sum(grad_out.astype(jnp.float32) * shared, axis=1))
    shared_cot = (switch[:, None] * grad_out.astype(jnp.float32)).astype(jnp.bfloat16)
    shared_hidden_grad = jnp.dot(shared_cot, shared_down.T, preferred_element_type=jnp.float32)
    shared_gate_part = (shared_hidden_grad * shared_pre_up * silu_grad(shared_pre_gate)).astype(jnp.bfloat16)
    shared_up_part = (shared_hidden_grad * jax.nn.silu(shared_pre_gate)).astype(jnp.bfloat16)
    shared_input_grad = jnp.dot(shared_gate_part, shared_gate.T, preferred_element_type=jnp.float32) + jnp.dot(shared_up_part, shared_up.T, preferred_element_type=jnp.float32)
    grad_tokens = (shared_input_grad + grad_sum + switch_grad[:, None] * shared_switch.astype(jnp.float32)[None, :]).astype(jnp.bfloat16)
    return (mixed, grad_tokens, gate_sum.reshape(TOKENS, TOPK))
```

```python
import jax
import jax.numpy as jnp
from jax import lax
from jax.experimental import pallas as pl
from jax.experimental.pallas import tpu as pltpu
from jax.sharding import PartitionSpec as P

AXES = ("tp", "ep")
LANES = 128
TILE = 16
VMEM = pltpu.VMEM
SMEM = pltpu.SMEM


def silu_grad(argument):
    gate_sig = jax.nn.sigmoid(argument)
    return gate_sig * (1.0 + argument * (1.0 - gate_sig))


def swap_matrix():
    size = TILE * TILE
    row = lax.broadcasted_iota(jnp.int32, (size, size), 0)
    col = lax.broadcasted_iota(jnp.int32, (size, size), 1)
    return jnp.where(((row & 15) * 16 + (row >> 4)) == col, 1.0, 0.0).astype(jnp.bfloat16)


def swap(perm, block):
    return jnp.dot(perm, block, preferred_element_type=jnp.float32).astype(jnp.bfloat16)


def columns_stacked(block):
    return jnp.concatenate(
        [block[:, j * LANES : (j + 1) * LANES] for j in range(TILE)], axis=0
    )


def rows_from_stack(stack):
    return jnp.concatenate([stack[j * TILE : (j + 1) * TILE] for j in range(TILE)], axis=1)


def pack_kernel(slot_ref, weight_ref, tokens_ref, cot_ref, out_ref, token_tiles, cot_tiles):
    perm = swap_matrix()
    count = tokens_ref.shape[0]
    zero = jnp.zeros((TILE, TILE, LANES), jnp.bfloat16)

    def clear(step, carry):
        out_ref[pl.ds(step * TILE, TILE)] = zero
        return carry

    lax.fori_loop(0, out_ref.shape[0] // TILE, clear, 0)
    for group in range(count // TILE):
        rows = slice(group * TILE, (group + 1) * TILE)
        both = jnp.concatenate(
            [columns_stacked(tokens_ref[rows, :]), columns_stacked(cot_ref[rows, :])], axis=1
        )
        both = swap(perm, both)
        token_tiles[rows] = both[:, :LANES].reshape(TILE, TILE, LANES)
        cot_tiles[rows] = both[:, LANES:].reshape(TILE, TILE, LANES)

    def place(token, carry):
        row = token_tiles[token]
        cot = cot_tiles[token].astype(jnp.float32)
        for k in range(2):
            slot = slot_ref[2 * token + k]
            at = (slot >> 1) * 4 + (slot & 1)
            out_ref[at] = row
            out_ref[at + 2] = (weight_ref[2 * token + k] * cot).astype(jnp.bfloat16)
        return carry

    lax.fori_loop(0, count, place, 0, unroll=4)


def pack(slots, weights, tokens, cot):
    count = tokens.shape[0]
    return pl.pallas_call(
        pack_kernel,
        out_shape=jax.ShapeDtypeStruct((1024, TILE, LANES), jnp.bfloat16),
        in_specs=[pl.BlockSpec(memory_space=SMEM)] * 2 + [pl.BlockSpec(memory_space=VMEM)] * 2,
        out_specs=pl.BlockSpec(memory_space=VMEM),
        scratch_shapes=[pltpu.VMEM((count, TILE, LANES), jnp.bfloat16)] * 2,
        compiler_params=pltpu.CompilerParams(vmem_limit_bytes=32 << 20),
        cost_estimate=pl.CostEstimate(
            flops=8 * 2 * 256**3, bytes_accessed=5 << 20, transcendentals=0
        ),
    )(slots, weights, tokens, cot)


def expert_kernel(got_ref, gate_ref, up_ref, down_ref, back_ref, rows, cots, outs, grads):
    perm = swap_matrix()
    count = rows.shape[0]

    def load(group, carry):
        tiles = got_ref[pl.ds(group * 32, 32)].reshape(8, 2, 2, TILE, LANES)
        both = jnp.concatenate(
            [tiles[:, 0].reshape(256, LANES), tiles[:, 1].reshape(256, LANES)], axis=1
        )
        both = swap(perm, both)
        at = pl.ds(pl.multiple_of(group * TILE, TILE), TILE)
        rows[at, :] = rows_from_stack(both[:, :LANES])
        cots[at, :] = rows_from_stack(both[:, LANES:])
        return carry

    lax.fori_loop(0, count // TILE, load, 0, unroll=2)
    one = (((1,), (0,)), ((), ()))
    other = (((1,), (1,)), ((), ()))

    def dot(a, b, dims):
        return lax.dot_general(a, b, dims, preferred_element_type=jnp.float32)

    pre_gate = dot(rows[...], gate_ref[...], one)
    pre_up = dot(rows[...], up_ref[...], one)
    sig = 1.0 / (1.0 + jnp.exp(-pre_gate))
    silu = pre_gate * sig
    hidden = (silu * pre_up).astype(jnp.bfloat16)
    outs[...] = dot(hidden, down_ref[...], one).astype(jnp.bfloat16)
    hidden_grad = dot(cots[...], down_ref[...], other)
    gate_part = (hidden_grad * pre_up * (sig * (1.0 + pre_gate * (1.0 - sig)))).astype(jnp.bfloat16)
    up_part = (hidden_grad * silu).astype(jnp.bfloat16)
    grads[...] = (dot(gate_part, gate_ref[...], other) + dot(up_part, up_ref[...], other)).astype(
        jnp.bfloat16
    )

    def store(group, carry):
        at = pl.ds(pl.multiple_of(group * TILE, TILE), TILE)
        both = jnp.concatenate(
            [columns_stacked(outs[at, :]), columns_stacked(grads[at, :])], axis=1
        )
        both = swap(perm, both)
        tiles = jnp.concatenate(
            [
                both[:, :LANES].reshape(8, 1, 2, TILE, LANES),
                both[:, LANES:].reshape(8, 1, 2, TILE, LANES),
            ],
            axis=1,
        )
        back_ref[pl.ds(group * 32, 32)] = tiles.reshape(32, TILE, LANES)
        return carry

    lax.fori_loop(0, count // TILE, store, 0, unroll=2)


def expert(got, gate, up, down):
    width, units = gate.shape
    steps = 2
    count = got.shape[0] // 2 // steps
    block = pl.BlockSpec((got.shape[0] // steps, TILE, LANES), lambda i: (i, 0, 0))

    def whole(array):
        return pl.BlockSpec(array.shape, lambda i: (0, 0), pipeline_mode=pl.Buffered(1))

    return pl.pallas_call(
        expert_kernel,
        out_shape=jax.ShapeDtypeStruct(got.shape, jnp.bfloat16),
        grid=(steps,),
        in_specs=[block, whole(gate), whole(up), whole(down)],
        out_specs=block,
        scratch_shapes=[pltpu.VMEM((count, width), jnp.bfloat16)] * 4,
        compiler_params=pltpu.CompilerParams(vmem_limit_bytes=50 << 20),
        cost_estimate=pl.CostEstimate(
            flops=512 * 2048 * 512 * 12, bytes_accessed=14 << 20, transcendentals=512 * 512
        ),
    )(got, gate, up, down)


def combine_kernel(
    slot_ref,
    weight_ref,
    rows_ref,
    cot_ref,
    shared_ref,
    shared_grad_ref,
    mixed_ref,
    grad_ref,
    gate_ref,
    mixed_tiles,
    grad_tiles,
    partial,
):
    perm = swap_matrix()
    count = cot_ref.shape[0]

    def gather(token, carry):
        cot = cot_ref[token].astype(jnp.float32)
        mixed = shared_ref[token]
        grad = shared_grad_ref[token]
        for k in range(2):
            slot = slot_ref[2 * token + k]
            at = (slot >> 1) * 4 + (slot & 1)
            output = rows_ref[at].astype(jnp.float32)
            mixed = mixed + weight_ref[2 * token + k] * output
            grad = grad + rows_ref[at + 2].astype(jnp.float32)
            partial[k, token] = jnp.sum((cot * output).reshape(2, 8, LANES), axis=0)
        mixed_tiles[token] = mixed.astype(jnp.bfloat16)
        grad_tiles[token] = grad.astype(jnp.bfloat16)
        return carry

    lax.fori_loop(0, count, gather, 0, unroll=4)
    for group in range(count // TILE):
        at = slice(group * TILE, (group + 1) * TILE)
        both = jnp.concatenate(
            [mixed_tiles[at].reshape(256, LANES), grad_tiles[at].reshape(256, LANES)], axis=1
        )
        both = swap(perm, both)
        mixed_ref[at, :] = rows_from_stack(both[:, :LANES])
        grad_ref[at, :] = rows_from_stack(both[:, LANES:])
    for k in range(2):
        gate_ref[:, k : k + 1] = jnp.sum(jnp.sum(partial[k], axis=1), axis=1, keepdims=True)


def combine(slots, weights, rows, cot, shared, shared_grad):
    count = cot.shape[0]
    width = TILE * LANES
    return pl.pallas_call(
        combine_kernel,
        out_shape=[
            jax.ShapeDtypeStruct((count, width), jnp.bfloat16),
            jax.ShapeDtypeStruct((count, width), jnp.bfloat16),
            jax.ShapeDtypeStruct((count, 2), jnp.float32),
        ],
        in_specs=[pl.BlockSpec(memory_space=SMEM)] * 2 + [pl.BlockSpec(memory_space=VMEM)] * 4,
        out_specs=[pl.BlockSpec(memory_space=VMEM)] * 3,
        scratch_shapes=[
            pltpu.VMEM((count, TILE, LANES), jnp.bfloat16),
            pltpu.VMEM((count, TILE, LANES), jnp.bfloat16),
            pltpu.VMEM((2, count, 8, LANES), jnp.float32),
        ],
        compiler_params=pltpu.CompilerParams(vmem_limit_bytes=32 << 20),
        cost_estimate=pl.CostEstimate(
            flops=8 * 2 * 256**3, bytes_accessed=8 << 20, transcendentals=0
        ),
    )(slots, weights, rows, cot, shared, shared_grad)


def route_slots(expert_ids):
    chosen = expert_ids.reshape(-1)
    number = jnp.arange(chosen.shape[0], dtype=jnp.int32)
    same = (chosen[:, None] == chosen[None, :]) & (number[None, :] < number[:, None])
    return chosen * 2 + jnp.sum(same.astype(jnp.int32), axis=1)


def shared_expert(tokens, grad_out, gate, up, down, switch_vector):
    def dot(a, b, spec):
        return jnp.einsum(spec, a, b, preferred_element_type=jnp.float32)

    switch = jax.nn.sigmoid(jnp.dot(tokens, switch_vector, preferred_element_type=jnp.float32))
    pre_gate = dot(tokens, gate, "td,df->tf")
    pre_up = dot(tokens, up, "td,df->tf")
    hidden = (jax.nn.silu(pre_gate) * pre_up).astype(jnp.bfloat16)
    shared = dot(hidden, down, "tf,fd->td")
    cot = grad_out.astype(jnp.float32)
    shared_cot = (switch[:, None] * cot).astype(jnp.bfloat16)
    hidden_grad = dot(shared_cot, down, "td,fd->tf")
    gate_part = (hidden_grad * pre_up * silu_grad(pre_gate)).astype(jnp.bfloat16)
    up_part = (hidden_grad * jax.nn.silu(pre_gate)).astype(jnp.bfloat16)
    input_grad = dot(gate_part, gate, "tf,df->td") + dot(up_part, up, "tf,df->td")
    switch_grad = switch * (1.0 - switch) * jnp.sum(cot * shared, axis=1)
    grad = input_grad + switch_grad[:, None] * switch_vector.astype(jnp.float32)[None, :]
    return switch[:, None] * shared, grad


def local(
    tokens,
    expert_ids,
    gate_weights,
    grad_out,
    expert_gate,
    expert_up,
    expert_down,
    shared_gate,
    shared_up,
    shared_down,
    shared_switch,
):
    devices = lax.axis_size("tp") * lax.axis_size("ep")
    tiled = (tokens.shape[0], TILE, LANES)
    slots = route_slots(expert_ids)
    weights = gate_weights.reshape(-1)
    sent = pack(slots, weights, tokens, grad_out)

    def exchange(rows):
        return lax.all_to_all(
            rows.reshape(devices, -1, LANES), AXES, split_axis=0, concat_axis=0, tiled=True
        ).reshape(rows.shape)

    got = exchange(sent)
    all_gate = lax.all_gather(shared_gate, "tp", axis=1, tiled=True)
    all_up = lax.all_gather(shared_up, "tp", axis=1, tiled=True)
    all_down = lax.all_gather(shared_down, "tp", axis=0, tiled=True)
    back = exchange(expert(got, expert_gate[0], expert_up[0], expert_down[0]))
    shared, shared_grad = shared_expert(
        tokens, grad_out, all_gate, all_up, all_down, shared_switch
    )
    mixed, grad_tokens, gate_grad = combine(
        slots,
        weights,
        back,
        grad_out.reshape(tiled),
        shared.reshape(tiled),
        shared_grad.reshape(tiled),
    )
    return (mixed, grad_tokens, gate_grad)


def solution(mesh):
    rows = P(AXES, None)
    experts = P(AXES, None, None)
    placed = (rows, rows, rows, rows, experts, experts, experts)
    placed += (P(None, "tp"), P(None, "tp"), P("tp", None), P())
    return jax.shard_map(
        local, mesh=mesh, in_specs=placed, out_specs=(rows, rows, rows), check_vma=False
    )
```

```python
import jax
import jax.numpy as jnp
from jax import lax
from jax.experimental import pallas as pl
from jax.experimental.pallas import tpu as pltpu
from jax.sharding import PartitionSpec as P

AXES = ("tp", "ep")
LANES = 128
TILE = 16
VMEM = pltpu.VMEM
SMEM = pltpu.SMEM


def silu_grad(argument):
    gate_sig = jax.nn.sigmoid(argument)
    return gate_sig * (1.0 + argument * (1.0 - gate_sig))


def swap_matrix():
    size = TILE * TILE
    row = lax.broadcasted_iota(jnp.int32, (size, size), 0)
    col = lax.broadcasted_iota(jnp.int32, (size, size), 1)
    return jnp.where(((row & 15) * 16 + (row >> 4)) == col, 1.0, 0.0).astype(jnp.bfloat16)


def swap(perm, block):
    return jnp.dot(perm, block, preferred_element_type=jnp.float32).astype(jnp.bfloat16)


def columns_stacked(block):
    return jnp.concatenate(
        [block[:, j * LANES : (j + 1) * LANES] for j in range(TILE)], axis=0
    )


def rows_from_stack(stack):
    return jnp.concatenate([stack[j * TILE : (j + 1) * TILE] for j in range(TILE)], axis=1)


def pack_kernel(slot_ref, weight_ref, tokens_ref, cot_ref, out_ref, token_tiles, cot_tiles):
    perm = swap_matrix()
    count = tokens_ref.shape[0]
    zero = jnp.zeros((TILE, TILE, LANES), jnp.bfloat16)

    def clear(step, carry):
        out_ref[pl.ds(step * TILE, TILE)] = zero
        return carry

    lax.fori_loop(0, out_ref.shape[0] // TILE, clear, 0)
    for group in range(count // TILE):
        rows = slice(group * TILE, (group + 1) * TILE)
        both = jnp.concatenate(
            [columns_stacked(tokens_ref[rows, :]), columns_stacked(cot_ref[rows, :])], axis=1
        )
        both = swap(perm, both)
        token_tiles[rows] = both[:, :LANES].reshape(TILE, TILE, LANES)
        cot_tiles[rows] = both[:, LANES:].reshape(TILE, TILE, LANES)

    def place(token, carry):
        row = token_tiles[token]
        cot = cot_tiles[token].astype(jnp.float32)
        for k in range(2):
            slot = slot_ref[k * count + token]
            at = (slot >> 1) * 4 + (slot & 1)
            out_ref[at] = row
            out_ref[at + 2] = (weight_ref[k * count + token] * cot).astype(jnp.bfloat16)
        return carry

    lax.fori_loop(0, count, place, 0, unroll=4)


def pack(slots, weights, tokens, cot):
    count = tokens.shape[0]
    return pl.pallas_call(
        pack_kernel,
        out_shape=jax.ShapeDtypeStruct((1024, TILE, LANES), jnp.bfloat16),
        in_specs=[pl.BlockSpec(memory_space=SMEM)] * 2 + [pl.BlockSpec(memory_space=VMEM)] * 2,
        out_specs=pl.BlockSpec(memory_space=VMEM),
        scratch_shapes=[pltpu.VMEM((count, TILE, LANES), jnp.bfloat16)] * 2,
        compiler_params=pltpu.CompilerParams(vmem_limit_bytes=32 << 20),
        cost_estimate=pl.CostEstimate(
            flops=8 * 2 * 256**3, bytes_accessed=5 << 20, transcendentals=0
        ),
    )(slots, weights, tokens, cot)


def expert_kernel(
    got_ref,
    gate_from,
    up_from,
    down_from,
    back_ref,
    rows,
    cots,
    outs,
    grads,
    gate_ref,
    up_ref,
    down_ref,
    arrived,
):
    perm = swap_matrix()
    count = rows.shape[0]
    copies = [
        pltpu.make_async_copy(gate_from, gate_ref, arrived.at[0]),
        pltpu.make_async_copy(up_from, up_ref, arrived.at[1]),
        pltpu.make_async_copy(down_from, down_ref, arrived.at[2]),
    ]

    @pl.when(pl.program_id(0) == 0)
    def _():
        for copy in copies:
            copy.start()

    def load(group, carry):
        tiles = got_ref[pl.ds(group * 32, 32)].reshape(8, 2, 2, TILE, LANES)
        both = jnp.concatenate(
            [tiles[:, 0].reshape(256, LANES), tiles[:, 1].reshape(256, LANES)], axis=1
        )
        both = swap(perm, both)
        at = pl.ds(pl.multiple_of(group * TILE, TILE), TILE)
        rows[at, :] = rows_from_stack(both[:, :LANES])
        cots[at, :] = rows_from_stack(both[:, LANES:])
        return carry

    lax.fori_loop(0, count // TILE, load, 0, unroll=True)

    @pl.when(pl.program_id(0) == 0)
    def _():
        for copy in copies:
            copy.wait()

    one = (((1,), (0,)), ((), ()))
    other = (((1,), (1,)), ((), ()))

    def dot(a, b, dims):
        return lax.dot_general(a, b, dims, preferred_element_type=jnp.float32)

    pre_gate = dot(rows[...], gate_ref[...], one)
    pre_up = dot(rows[...], up_ref[...], one)
    sig = 1.0 / (1.0 + jnp.exp(-pre_gate))
    silu = pre_gate * sig
    hidden = (silu * pre_up).astype(jnp.bfloat16)
    outs[...] = dot(hidden, down_ref[...], one).astype(jnp.bfloat16)
    hidden_grad = dot(cots[...], down_ref[...], other)
    gate_part = (hidden_grad * pre_up * (sig * (1.0 + pre_gate * (1.0 - sig)))).astype(jnp.bfloat16)
    up_part = (hidden_grad * silu).astype(jnp.bfloat16)
    grads[...] = (dot(gate_part, gate_ref[...], other) + dot(up_part, up_ref[...], other)).astype(
        jnp.bfloat16
    )

    def store(group, carry):
        at = pl.ds(pl.multiple_of(group * TILE, TILE), TILE)
        both = jnp.concatenate(
            [columns_stacked(outs[at, :]), columns_stacked(grads[at, :])], axis=1
        )
        both = swap(perm, both)
        tiles = jnp.concatenate(
            [
                both[:, :LANES].reshape(8, 1, 2, TILE, LANES),
                both[:, LANES:].reshape(8, 1, 2, TILE, LANES),
            ],
            axis=1,
        )
        back_ref[pl.ds(group * 32, 32)] = tiles.reshape(32, TILE, LANES)
        return carry

    lax.fori_loop(0, count // TILE, store, 0, unroll=True)


def expert(got, gate, up, down):
    width, units = gate.shape
    steps = 2
    count = got.shape[0] // 2 // steps
    block = pl.BlockSpec((got.shape[0] // steps, TILE, LANES), lambda i: (i, 0, 0))

    weights = [gate, up, down]
    return pl.pallas_call(
        expert_kernel,
        out_shape=jax.ShapeDtypeStruct(got.shape, jnp.bfloat16),
        grid=(steps,),
        in_specs=[block] + [pl.BlockSpec(memory_space=pl.ANY)] * 3,
        out_specs=block,
        scratch_shapes=[pltpu.VMEM((count, width), jnp.bfloat16)] * 4
        + [pltpu.VMEM(w.shape, jnp.bfloat16) for w in weights]
        + [pltpu.SemaphoreType.DMA((3,))],
        compiler_params=pltpu.CompilerParams(vmem_limit_bytes=50 << 20),
        cost_estimate=pl.CostEstimate(
            flops=512 * 2048 * 512 * 12, bytes_accessed=14 << 20, transcendentals=512 * 512
        ),
    )(got, *weights)


def combine_kernel(
    slot_ref,
    weight_ref,
    rows_ref,
    cot_ref,
    shared_ref,
    shared_grad_ref,
    mixed_ref,
    grad_ref,
    gate_ref,
    mixed_tiles,
    grad_tiles,
    partial,
):
    perm = swap_matrix()
    count = cot_ref.shape[0]

    def gather(token, carry):
        cot = cot_ref[token].astype(jnp.float32)
        mixed = shared_ref[token]
        grad = shared_grad_ref[token]
        for k in range(2):
            slot = slot_ref[k * count + token]
            at = (slot >> 1) * 4 + (slot & 1)
            output = rows_ref[at].astype(jnp.float32)
            mixed = mixed + weight_ref[k * count + token] * output
            grad = grad + rows_ref[at + 2].astype(jnp.float32)
            partial[k, token] = jnp.sum((cot * output).reshape(2, 8, LANES), axis=0)
        mixed_tiles[token] = mixed.astype(jnp.bfloat16)
        grad_tiles[token] = grad.astype(jnp.bfloat16)
        return carry

    lax.fori_loop(0, count, gather, 0, unroll=4)
    for group in range(count // TILE):
        at = slice(group * TILE, (group + 1) * TILE)
        both = jnp.concatenate(
            [mixed_tiles[at].reshape(256, LANES), grad_tiles[at].reshape(256, LANES)], axis=1
        )
        both = swap(perm, both)
        mixed_ref[at, :] = rows_from_stack(both[:, :LANES])
        grad_ref[at, :] = rows_from_stack(both[:, LANES:])
    for k in range(2):
        gate_ref[:, k : k + 1] = jnp.sum(jnp.sum(partial[k], axis=1), axis=1, keepdims=True)


def combine(slots, weights, rows, cot, shared, shared_grad):
    count = cot.shape[0]
    width = TILE * LANES
    return pl.pallas_call(
        combine_kernel,
        out_shape=[
            jax.ShapeDtypeStruct((count, width), jnp.bfloat16),
            jax.ShapeDtypeStruct((count, width), jnp.bfloat16),
            jax.ShapeDtypeStruct((count, 2), jnp.float32),
        ],
        in_specs=[pl.BlockSpec(memory_space=SMEM)] * 2 + [pl.BlockSpec(memory_space=VMEM)] * 4,
        out_specs=[pl.BlockSpec(memory_space=VMEM)] * 3,
        scratch_shapes=[
            pltpu.VMEM((count, TILE, LANES), jnp.bfloat16),
            pltpu.VMEM((count, TILE, LANES), jnp.bfloat16),
            pltpu.VMEM((2, count, 8, LANES), jnp.float32),
        ],
        compiler_params=pltpu.CompilerParams(vmem_limit_bytes=32 << 20),
        cost_estimate=pl.CostEstimate(
            flops=8 * 2 * 256**3, bytes_accessed=8 << 20, transcendentals=0
        ),
    )(slots, weights, rows, cot, shared, shared_grad)


def route_slots(expert_ids):
    chosen = expert_ids.T.reshape(-1)
    number = jnp.arange(chosen.shape[0], dtype=jnp.int32)
    same = (chosen[:, None] == chosen[None, :]) & (number[None, :] < number[:, None])
    return chosen * 2 + jnp.sum(same.astype(jnp.int32), axis=1)


def shared_expert(tokens, grad_out, gate, up, down, switch_vector):
    def dot(a, b, spec):
        return jnp.einsum(spec, a, b, preferred_element_type=jnp.float32)

    switch = jax.nn.sigmoid(jnp.dot(tokens, switch_vector, preferred_element_type=jnp.float32))
    pre_gate = dot(tokens, gate, "td,df->tf")
    pre_up = dot(tokens, up, "td,df->tf")
    hidden = (jax.nn.silu(pre_gate) * pre_up).astype(jnp.bfloat16)
    shared = dot(hidden, down, "tf,fd->td")
    cot = grad_out.astype(jnp.float32)
    shared_cot = (switch[:, None] * cot).astype(jnp.bfloat16)
    hidden_grad = dot(shared_cot, down, "td,fd->tf")
    gate_part = (hidden_grad * pre_up * silu_grad(pre_gate)).astype(jnp.bfloat16)
    up_part = (hidden_grad * jax.nn.silu(pre_gate)).astype(jnp.bfloat16)
    input_grad = dot(gate_part, gate, "tf,df->td") + dot(up_part, up, "tf,df->td")
    switch_grad = switch * (1.0 - switch) * jnp.sum(cot * shared, axis=1)
    grad = input_grad + switch_grad[:, None] * switch_vector.astype(jnp.float32)[None, :]
    return switch[:, None] * shared, grad


def local(
    tokens,
    expert_ids,
    gate_weights,
    grad_out,
    expert_gate,
    expert_up,
    expert_down,
    shared_gate,
    shared_up,
    shared_down,
    shared_switch,
):
    devices = lax.axis_size("tp") * lax.axis_size("ep")
    tiled = (tokens.shape[0], TILE, LANES)
    slots = route_slots(expert_ids)
    weights = gate_weights.T.reshape(-1)
    sent = pack(slots, weights, tokens, grad_out)

    def exchange(rows):
        return lax.all_to_all(
            rows.reshape(devices, -1, LANES), AXES, split_axis=0, concat_axis=0, tiled=True
        ).reshape(rows.shape)

    got = exchange(sent)
    all_in = lax.all_gather(
        jnp.concatenate([shared_gate, shared_up], axis=0), "tp", axis=1, tiled=True
    )
    got, all_in, shared_down = lax.optimization_barrier((got, all_in, shared_down))
    all_gate, all_up = jnp.split(all_in, 2, axis=0)
    all_down = lax.all_gather(shared_down, "tp", axis=0, tiled=True)
    back = exchange(expert(got, expert_gate[0], expert_up[0], expert_down[0]))
    shared, shared_grad = shared_expert(
        tokens, grad_out, all_gate, all_up, all_down, shared_switch
    )
    mixed, grad_tokens, gate_grad = combine(
        slots,
        weights,
        back,
        grad_out.reshape(tiled),
        shared.reshape(tiled),
        shared_grad.reshape(tiled),
    )
    return (mixed, grad_tokens, gate_grad)


def solution(mesh):
    rows = P(AXES, None)
    experts = P(AXES, None, None)
    placed = (rows, rows, rows, rows, experts, experts, experts)
    placed += (P(None, "tp"), P(None, "tp"), P("tp", None), P())
    return jax.shard_map(
        local, mesh=mesh, in_specs=placed, out_specs=(rows, rows, rows), check_vma=False
    )
```

```python
import jax
import jax.numpy as jnp
from jax import lax
from jax.experimental import pallas as pl
from jax.experimental.pallas import tpu as pltpu
from jax.sharding import PartitionSpec as P

AXES = ("tp", "ep")
LANES = 128
TILE = 16
VMEM = pltpu.VMEM
SMEM = pltpu.SMEM
HBM = pltpu.HBM
PARTS = 4


def silu_grad(argument):
    gate_sig = jax.nn.sigmoid(argument)
    return gate_sig * (1.0 + argument * (1.0 - gate_sig))


def swap_matrix():
    size = TILE * TILE
    row = lax.broadcasted_iota(jnp.int32, (size, size), 0)
    col = lax.broadcasted_iota(jnp.int32, (size, size), 1)
    return jnp.where(((row & 15) * 16 + (row >> 4)) == col, 1.0, 0.0).astype(jnp.bfloat16)


def swap(perm, block):
    return jnp.dot(perm, block, preferred_element_type=jnp.float32).astype(jnp.bfloat16)


def columns_stacked(block):
    return jnp.concatenate(
        [block[:, j * LANES : (j + 1) * LANES] for j in range(TILE)], axis=0
    )


def rows_from_stack(stack):
    return jnp.concatenate([stack[j * TILE : (j + 1) * TILE] for j in range(TILE)], axis=1)


def pack_kernel(
    chosen_ref, weight_ref, tokens_from, cot_from, out_ref, tokens, cots, token_tiles, cot_tiles,
    first, second, moved
):
    came = [
        pltpu.make_async_copy(tokens_from, tokens, moved.at[0]),
        pltpu.make_async_copy(cot_from, cots, moved.at[1]),
    ]
    for copy in came:
        copy.start()
    perm = swap_matrix()
    count = tokens.shape[0]
    zero = jnp.zeros((8, 2, TILE, LANES), jnp.bfloat16)

    def clear(step, carry):
        first[pl.ds(step * 8, 8)] = zero
        second[pl.ds(step * 8, 8)] = zero
        return carry

    lax.fori_loop(0, first.shape[0] // 8, clear, 0, unroll=4)
    for copy in came:
        copy.wait()
    for group in range(count // TILE):
        rows = slice(group * TILE, (group + 1) * TILE)
        both = jnp.concatenate(
            [columns_stacked(tokens[rows, :]), columns_stacked(cots[rows, :])], axis=1
        )
        both = swap(perm, both)
        token_tiles[rows] = both[:, :LANES].reshape(TILE, TILE, LANES)
        cot_tiles[rows] = both[:, LANES:].reshape(TILE, TILE, LANES)

    def place(slot, order, backward):
        def step(number, carry):
            token = count - 1 - number if backward else number
            row = token_tiles[token]
            cot = cot_tiles[token].astype(jnp.float32)
            for k in order:
                at = chosen_ref[k * count + token]
                slot[at, 0] = row
                slot[at, 1] = (weight_ref[k * count + token] * cot).astype(jnp.bfloat16)
            return carry

        lax.fori_loop(0, count, step, 0, unroll=4)

    gone = [
        pltpu.make_async_copy(first, out_ref.at[:, 0], moved.at[2]),
        pltpu.make_async_copy(second, out_ref.at[:, 1], moved.at[3]),
    ]
    place(first, (0, 1), False)
    gone[0].start()
    place(second, (1, 0), True)
    gone[1].start()
    for copy in gone:
        copy.wait()


def pack(chosen, weights, tokens, cot, experts):
    count = tokens.shape[0]
    return pl.pallas_call(
        pack_kernel,
        out_shape=jax.ShapeDtypeStruct((experts, 2, 2, TILE, LANES), jnp.bfloat16),
        in_specs=[pl.BlockSpec(memory_space=SMEM)] * 2 + [pl.BlockSpec(memory_space=HBM)] * 2,
        out_specs=pl.BlockSpec(memory_space=HBM),
        scratch_shapes=[pltpu.VMEM(tokens.shape, jnp.bfloat16)] * 2
        + [pltpu.VMEM((count, TILE, LANES), jnp.bfloat16)] * 2
        + [pltpu.VMEM((experts, 2, TILE, LANES), jnp.bfloat16)] * 2
        + [pltpu.SemaphoreType.DMA((4,))],
        compiler_params=pltpu.CompilerParams(vmem_limit_bytes=32 << 20),
        cost_estimate=pl.CostEstimate(
            flops=8 * 2 * 256**3, bytes_accessed=5 << 20, transcendentals=0
        ),
    )(chosen, weights, tokens, cot)


def expert_kernel(
    got_from, gate_from, up_from, down_from, back_to, got, back, rows, cots, outs, grads, gate_ref,
    up_ref, down_ref, arrived, came, gone
):
    perm = swap_matrix()
    blocks, count, width = rows.shape
    weights = [
        pltpu.make_async_copy(gate_from, gate_ref, arrived.at[0]),
        pltpu.make_async_copy(up_from, up_ref, arrived.at[1]),
        pltpu.make_async_copy(down_from, down_ref, arrived.at[2]),
    ]
    total = blocks * PARTS
    size = blocks * count // total
    groups = size // TILE

    def part(ref, number):
        return ref.at[pl.ds(number * size, size)]

    def load_copy(number):
        return pltpu.make_async_copy(part(got_from, number), part(got, number), came.at[number])

    def store_copy(number):
        return pltpu.make_async_copy(part(back, number), part(back_to, number), gone.at[number])

    load_copy(0).start()
    for copy in weights[:2]:
        copy.start()
    for number in range(1, total):
        load_copy(number).start()
    weights[2].start()
    one = (((1,), (0,)), ((), ()))
    other = (((1,), (1,)), ((), ()))

    def dot(a, b, dims):
        return lax.dot_general(a, b, dims, preferred_element_type=jnp.float32)

    for block in range(blocks):
        for number in range(block * PARTS, (block + 1) * PARTS):
            load_copy(number).wait()
            for group in range(groups):
                at = number * size + group * TILE
                tiles = got[at : at + TILE]
                both = jnp.concatenate(
                    [tiles[:, 0].reshape(256, LANES), tiles[:, 1].reshape(256, LANES)], axis=1
                )
                both = swap(perm, both)
                to = slice(at - block * count, at - block * count + TILE)
                rows[block, to, :] = rows_from_stack(both[:, :LANES])
                cots[block, to, :] = rows_from_stack(both[:, LANES:])
        if block == 0:
            weights[0].wait()
            weights[1].wait()
        pre_gate = dot(rows[block], gate_ref[...], one)
        pre_up = dot(rows[block], up_ref[...], one)
        sig = 1.0 / (1.0 + jnp.exp(-pre_gate))
        silu = pre_gate * sig
        hidden = (silu * pre_up).astype(jnp.bfloat16)
        if block == 0:
            weights[2].wait()
        outs[block] = dot(hidden, down_ref[...], one).astype(jnp.bfloat16)
        hidden_grad = dot(cots[block], down_ref[...], other)
        gate_part = hidden_grad * pre_up * (sig * (1.0 + pre_gate * (1.0 - sig)))
        gate_part = gate_part.astype(jnp.bfloat16)
        up_part = (hidden_grad * silu).astype(jnp.bfloat16)
        grads[block] = (
            dot(gate_part, gate_ref[...], other) + dot(up_part, up_ref[...], other)
        ).astype(jnp.bfloat16)
        for number in range(block * PARTS, (block + 1) * PARTS):
            for group in range(groups):
                at = number * size + group * TILE
                to = slice(at - block * count, at - block * count + TILE)
                both = jnp.concatenate(
                    [columns_stacked(outs[block, to, :]), columns_stacked(grads[block, to, :])],
                    axis=1,
                )
                both = swap(perm, both)
                back[at : at + TILE, 0] = both[:, :LANES].reshape(TILE, TILE, LANES)
                back[at : at + TILE, 1] = both[:, LANES:].reshape(TILE, TILE, LANES)
            store_copy(number).start()
    for number in range(total):
        store_copy(number).wait()


def expert(got, gate, up, down):
    blocks = 2
    count = got.shape[0] // blocks
    weights = [gate, up, down]
    return pl.pallas_call(
        expert_kernel,
        out_shape=jax.ShapeDtypeStruct(got.shape, jnp.bfloat16),
        in_specs=[pl.BlockSpec(memory_space=HBM)] * 4,
        out_specs=pl.BlockSpec(memory_space=HBM),
        scratch_shapes=[pltpu.VMEM(got.shape, jnp.bfloat16)] * 2
        + [pltpu.VMEM((blocks, count, gate.shape[0]), jnp.bfloat16)] * 4
        + [pltpu.VMEM(w.shape, jnp.bfloat16) for w in weights]
        + [pltpu.SemaphoreType.DMA((3,))]
        + [pltpu.SemaphoreType.DMA((blocks * PARTS,))] * 2,
        compiler_params=pltpu.CompilerParams(vmem_limit_bytes=50 << 20),
        cost_estimate=pl.CostEstimate(
            flops=512 * 2048 * 512 * 12, bytes_accessed=14 << 20, transcendentals=512 * 512
        ),
    )(got, *weights)


def combine_kernel(
    slot_ref, weight_ref, rows_from, cot_ref, shared_ref, shared_grad_ref, mixed_ref, grad_ref,
    gate_ref, outputs, grads, mixed_tiles, grad_tiles, partial, came
):
    copies = [
        pltpu.make_async_copy(rows_from.at[:, 0], outputs, came.at[0]),
        pltpu.make_async_copy(rows_from.at[:, 1], grads, came.at[1]),
    ]
    for copy in copies:
        copy.start()
    perm = swap_matrix()
    count = cot_ref.shape[0]

    def gather_output(token, carry):
        cot = cot_ref[token].astype(jnp.float32)
        mixed = shared_ref[token]
        for k in range(2):
            output = outputs[slot_ref[k * count + token]].astype(jnp.float32)
            mixed = mixed + weight_ref[k * count + token] * output
            partial[k, token] = jnp.sum((cot * output).reshape(2, 8, LANES), axis=0)
        mixed_tiles[token] = mixed.astype(jnp.bfloat16)
        return carry

    def gather_grad(token, carry):
        grad = shared_grad_ref[token]
        for k in range(2):
            grad = grad + grads[slot_ref[k * count + token]].astype(jnp.float32)
        grad_tiles[token] = grad.astype(jnp.bfloat16)
        return carry

    copies[0].wait()
    lax.fori_loop(0, count, gather_output, 0, unroll=4)
    copies[1].wait()
    lax.fori_loop(0, count, gather_grad, 0, unroll=4)
    for group in range(count // TILE):
        at = slice(group * TILE, (group + 1) * TILE)
        both = jnp.concatenate(
            [mixed_tiles[at].reshape(256, LANES), grad_tiles[at].reshape(256, LANES)], axis=1
        )
        both = swap(perm, both)
        mixed_ref[at, :] = rows_from_stack(both[:, :LANES])
        grad_ref[at, :] = rows_from_stack(both[:, LANES:])
    ones = jnp.ones((8, LANES), jnp.float32)
    for k in range(2):
        sums = lax.dot_general(
            ones,
            jnp.sum(partial[k], axis=1),
            (((1,), (1,)), ((), ())),
            precision=lax.Precision.HIGHEST,
            preferred_element_type=jnp.float32,
        )
        gate_ref[k : k + 1, :] = sums[:1]


def combine(slots, weights, rows, cot, shared, shared_grad):
    count = cot.shape[0]
    width = TILE * LANES
    return pl.pallas_call(
        combine_kernel,
        out_shape=[
            jax.ShapeDtypeStruct((count, width), jnp.bfloat16),
            jax.ShapeDtypeStruct((count, width), jnp.bfloat16),
            jax.ShapeDtypeStruct((2, count), jnp.float32),
        ],
        in_specs=[pl.BlockSpec(memory_space=SMEM)] * 2
        + [pl.BlockSpec(memory_space=HBM)]
        + [pl.BlockSpec(memory_space=VMEM)] * 3,
        out_specs=[pl.BlockSpec(memory_space=VMEM)] * 3,
        scratch_shapes=[
            pltpu.VMEM((rows.shape[0], TILE, LANES), jnp.bfloat16),
            pltpu.VMEM((rows.shape[0], TILE, LANES), jnp.bfloat16),
            pltpu.VMEM((count, TILE, LANES), jnp.bfloat16),
            pltpu.VMEM((count, TILE, LANES), jnp.bfloat16),
            pltpu.VMEM((2, count, 8, LANES), jnp.float32),
            pltpu.SemaphoreType.DMA((2,)),
        ],
        compiler_params=pltpu.CompilerParams(vmem_limit_bytes=32 << 20),
        cost_estimate=pl.CostEstimate(
            flops=8 * 2 * 256**3, bytes_accessed=8 << 20, transcendentals=0
        ),
    )(slots, weights, rows, cot, shared, shared_grad)


def route_slots(chosen, count):
    number = jnp.arange(chosen.shape[0], dtype=jnp.int32)
    written = 2 * (number % count) + number // count
    same = (chosen[:, None] == chosen[None, :]) & (written[None, :] > written[:, None])
    return chosen * 2 + jnp.sum(same.astype(jnp.int32), axis=1)


def shared_expert(tokens, grad_out, gate, up, down, switch_vector):
    def dot(a, b, spec):
        return jnp.einsum(spec, a, b, preferred_element_type=jnp.float32)

    switch = jax.nn.sigmoid(jnp.dot(tokens, switch_vector, preferred_element_type=jnp.float32))
    pre_gate = dot(tokens, gate, "td,df->tf")
    pre_up = dot(tokens, up, "td,df->tf")
    hidden = (jax.nn.silu(pre_gate) * pre_up).astype(jnp.bfloat16)
    shared = dot(hidden, down, "tf,fd->td")
    cot = grad_out.astype(jnp.float32)
    shared_cot = (switch[:, None] * cot).astype(jnp.bfloat16)
    hidden_grad = dot(shared_cot, down, "td,fd->tf")
    gate_part = (hidden_grad * pre_up * silu_grad(pre_gate)).astype(jnp.bfloat16)
    up_part = (hidden_grad * jax.nn.silu(pre_gate)).astype(jnp.bfloat16)
    input_grad = dot(gate_part, gate, "tf,df->td") + dot(up_part, up, "tf,df->td")
    switch_grad = switch * (1.0 - switch) * jnp.sum(cot * shared, axis=1)
    grad = input_grad + switch_grad[:, None] * switch_vector.astype(jnp.float32)[None, :]
    return switch[:, None] * shared, grad


def local(
    tokens,
    expert_ids,
    gate_weights,
    grad_out,
    expert_gate,
    expert_up,
    expert_down,
    shared_gate,
    shared_up,
    shared_down,
    shared_switch,
):
    devices = lax.axis_size("tp") * lax.axis_size("ep")
    count = tokens.shape[0]
    tiled = (count, TILE, LANES)
    chosen = expert_ids.T.reshape(-1)
    weights = gate_weights.T.reshape(-1)
    sent = pack(chosen, weights, tokens, grad_out, devices)

    def exchange(rows):
        return lax.all_to_all(
            rows.reshape(devices, -1, LANES), AXES, split_axis=0, concat_axis=0, tiled=True
        ).reshape(2 * devices, 2, TILE, LANES)

    got = exchange(sent)
    all_in = lax.all_gather(
        jnp.concatenate([shared_gate, shared_up], axis=0), "tp", axis=1, tiled=True
    )
    got, all_in, shared_down, routes = lax.optimization_barrier((got, all_in, shared_down, chosen))
    all_gate, all_up = jnp.split(all_in, 2, axis=0)
    all_down = lax.all_gather(shared_down, "tp", axis=0, tiled=True)
    back = exchange(expert(got, expert_gate[0], expert_up[0], expert_down[0]))
    shared, shared_grad = shared_expert(
        tokens, grad_out, all_gate, all_up, all_down, shared_switch
    )
    mixed, grad_tokens, gate_grad = combine(
        route_slots(routes, count),
        weights,
        back,
        grad_out.reshape(tiled),
        shared.reshape(tiled),
        shared_grad.reshape(tiled),
    )
    return (mixed, grad_tokens, gate_grad.T)


def solution(mesh):
    rows = P(AXES, None)
    experts = P(AXES, None, None)
    placed = (rows, rows, rows, rows, experts, experts, experts)
    placed += (P(None, "tp"), P(None, "tp"), P("tp", None), P())
    return jax.shard_map(
        local, mesh=mesh, in_specs=placed, out_specs=(rows, rows, rows), check_vma=False
    )
```

```python
import jax
import jax.numpy as jnp
from jax import lax
from jax.experimental import pallas as pl
from jax.experimental.pallas import tpu as pltpu
from jax.sharding import PartitionSpec as P

AXES = ("tp", "ep")
LANES = 128
TILE = 16
VMEM = pltpu.VMEM
SMEM = pltpu.SMEM
HBM = pltpu.HBM
PARTS = 4


def silu_grad(argument):
    gate_sig = jax.nn.sigmoid(argument)
    return gate_sig * (1.0 + argument * (1.0 - gate_sig))


def swap_matrix():
    size = TILE * TILE
    row = lax.broadcasted_iota(jnp.int32, (size, size), 0)
    col = lax.broadcasted_iota(jnp.int32, (size, size), 1)
    return jnp.where(((row & 15) * 16 + (row >> 4)) == col, 1.0, 0.0).astype(jnp.bfloat16)


def swap(perm, block):
    return jnp.dot(perm, block, preferred_element_type=jnp.float32).astype(jnp.bfloat16)


def columns_stacked(block):
    return jnp.concatenate(
        [block[:, j * LANES : (j + 1) * LANES] for j in range(TILE)], axis=0
    )


def rows_from_stack(stack):
    return jnp.concatenate([stack[j * TILE : (j + 1) * TILE] for j in range(TILE)], axis=1)


def pack_kernel(
    chosen_ref, weight_ref, tokens_from, cot_from, out_ref, tokens, cots, token_tiles, cot_tiles,
    first, second, moved
):
    came = [
        pltpu.make_async_copy(tokens_from, tokens, moved.at[0]),
        pltpu.make_async_copy(cot_from, cots, moved.at[1]),
    ]
    for copy in came:
        copy.start()
    perm = swap_matrix()
    count = tokens.shape[0]
    zero = jnp.zeros((8, 2, TILE, LANES), jnp.bfloat16)

    def clear(step, carry):
        first[pl.ds(step * 8, 8)] = zero
        second[pl.ds(step * 8, 8)] = zero
        return carry

    lax.fori_loop(0, first.shape[0] // 8, clear, 0, unroll=4)
    for copy in came:
        copy.wait()
    for group in range(count // TILE):
        rows = slice(group * TILE, (group + 1) * TILE)
        both = jnp.concatenate(
            [columns_stacked(tokens[rows, :]), columns_stacked(cots[rows, :])], axis=1
        )
        both = swap(perm, both)
        token_tiles[rows] = both[:, :LANES].reshape(TILE, TILE, LANES)
        cot_tiles[rows] = both[:, LANES:].reshape(TILE, TILE, LANES)

    def place(slot, order, backward):
        def step(number, carry):
            token = count - 1 - number if backward else number
            row = token_tiles[token]
            cot = cot_tiles[token].astype(jnp.float32)
            for k in order:
                at = chosen_ref[k * count + token]
                slot[at, 0] = row
                slot[at, 1] = (weight_ref[k * count + token] * cot).astype(jnp.bfloat16)
            return carry

        lax.fori_loop(0, count, step, 0, unroll=4)

    gone = [
        pltpu.make_async_copy(first, out_ref.at[:, 0], moved.at[2]),
        pltpu.make_async_copy(second, out_ref.at[:, 1], moved.at[3]),
    ]
    place(first, (0, 1), False)
    gone[0].start()
    place(second, (1, 0), True)
    gone[1].start()
    for copy in gone:
        copy.wait()


def pack(chosen, weights, tokens, cot, experts):
    count = tokens.shape[0]
    return pl.pallas_call(
        pack_kernel,
        out_shape=jax.ShapeDtypeStruct((experts, 2, 2, TILE, LANES), jnp.bfloat16),
        in_specs=[pl.BlockSpec(memory_space=SMEM)] * 2 + [pl.BlockSpec(memory_space=HBM)] * 2,
        out_specs=pl.BlockSpec(memory_space=HBM),
        scratch_shapes=[pltpu.VMEM(tokens.shape, jnp.bfloat16)] * 2
        + [pltpu.VMEM((count, TILE, LANES), jnp.bfloat16)] * 2
        + [pltpu.VMEM((experts, 2, TILE, LANES), jnp.bfloat16)] * 2
        + [pltpu.SemaphoreType.DMA((4,))],
        compiler_params=pltpu.CompilerParams(vmem_limit_bytes=60 << 20),
        cost_estimate=pl.CostEstimate(
            flops=8 * 2 * 256**3, bytes_accessed=5 << 20, transcendentals=0
        ),
    )(chosen, weights, tokens, cot)


def expert_kernel(
    got_from, gate_from, up_from, down_from, back_to, got, back, rows, cots, outs, grads, gate_ref,
    up_ref, down_ref, arrived, came, gone
):
    perm = swap_matrix()
    blocks, count, width = rows.shape
    weights = [
        pltpu.make_async_copy(gate_from, gate_ref, arrived.at[0]),
        pltpu.make_async_copy(up_from, up_ref, arrived.at[1]),
        pltpu.make_async_copy(down_from, down_ref, arrived.at[2]),
    ]
    total = blocks * PARTS
    size = blocks * count // total
    groups = size // TILE

    def part(ref, number):
        return ref.at[pl.ds(number * size, size)]

    def load_copy(number):
        return pltpu.make_async_copy(part(got_from, number), part(got, number), came.at[number])

    def store_copy(number):
        return pltpu.make_async_copy(part(back, number), part(back_to, number), gone.at[number])

    load_copy(0).start()
    for copy in weights[:2]:
        copy.start()
    for number in range(1, total):
        load_copy(number).start()
    weights[2].start()
    one = (((1,), (0,)), ((), ()))
    other = (((1,), (1,)), ((), ()))

    def dot(a, b, dims):
        return lax.dot_general(a, b, dims, preferred_element_type=jnp.float32)

    for block in range(blocks):
        for number in range(block * PARTS, (block + 1) * PARTS):
            load_copy(number).wait()
            for group in range(groups):
                at = number * size + group * TILE
                tiles = got[at : at + TILE]
                both = jnp.concatenate(
                    [tiles[:, 0].reshape(256, LANES), tiles[:, 1].reshape(256, LANES)], axis=1
                )
                both = swap(perm, both)
                to = slice(at - block * count, at - block * count + TILE)
                rows[block, to, :] = rows_from_stack(both[:, :LANES])
                cots[block, to, :] = rows_from_stack(both[:, LANES:])
        if block == 0:
            weights[0].wait()
            weights[1].wait()
        pre_gate = dot(rows[block], gate_ref[...], one)
        pre_up = dot(rows[block], up_ref[...], one)
        sig = 1.0 / (1.0 + jnp.exp(-pre_gate))
        silu = pre_gate * sig
        hidden = (silu * pre_up).astype(jnp.bfloat16)
        if block == 0:
            weights[2].wait()
        outs[block] = dot(hidden, down_ref[...], one).astype(jnp.bfloat16)
        hidden_grad = dot(cots[block], down_ref[...], other)
        gate_part = hidden_grad * pre_up * (sig * (1.0 + pre_gate * (1.0 - sig)))
        gate_part = gate_part.astype(jnp.bfloat16)
        up_part = (hidden_grad * silu).astype(jnp.bfloat16)
        grads[block] = (
            dot(gate_part, gate_ref[...], other) + dot(up_part, up_ref[...], other)
        ).astype(jnp.bfloat16)
        for number in range(block * PARTS, (block + 1) * PARTS):
            for group in range(groups):
                at = number * size + group * TILE
                to = slice(at - block * count, at - block * count + TILE)
                both = jnp.concatenate(
                    [columns_stacked(outs[block, to, :]), columns_stacked(grads[block, to, :])],
                    axis=1,
                )
                both = swap(perm, both)
                back[at : at + TILE, 0] = both[:, :LANES].reshape(TILE, TILE, LANES)
                back[at : at + TILE, 1] = both[:, LANES:].reshape(TILE, TILE, LANES)
            store_copy(number).start()
    for number in range(total):
        store_copy(number).wait()


def expert(got, gate, up, down):
    blocks = 2
    count = got.shape[0] // blocks
    weights = [gate, up, down]
    return pl.pallas_call(
        expert_kernel,
        out_shape=jax.ShapeDtypeStruct(got.shape, jnp.bfloat16),
        in_specs=[pl.BlockSpec(memory_space=HBM)] * 4,
        out_specs=pl.BlockSpec(memory_space=HBM),
        scratch_shapes=[pltpu.VMEM(got.shape, jnp.bfloat16)] * 2
        + [pltpu.VMEM((blocks, count, gate.shape[0]), jnp.bfloat16)] * 4
        + [pltpu.VMEM(w.shape, jnp.bfloat16) for w in weights]
        + [pltpu.SemaphoreType.DMA((3,))]
        + [pltpu.SemaphoreType.DMA((blocks * PARTS,))] * 2,
        compiler_params=pltpu.CompilerParams(vmem_limit_bytes=50 << 20),
        cost_estimate=pl.CostEstimate(
            flops=512 * 2048 * 512 * 12, bytes_accessed=14 << 20, transcendentals=512 * 512
        ),
    )(got, *weights)


def combine_kernel(
    slot_ref, weight_ref, rows_from, cot_ref, shared_ref, shared_grad_ref, mixed_ref, grad_ref,
    gate_ref, outputs, grads, mixed_tiles, grad_tiles, partial, came
):
    copies = [
        pltpu.make_async_copy(rows_from.at[:, 0], outputs, came.at[0]),
        pltpu.make_async_copy(rows_from.at[:, 1], grads, came.at[1]),
    ]
    for copy in copies:
        copy.start()
    perm = swap_matrix()
    count = cot_ref.shape[0]

    def gather_output(token, carry):
        cot = cot_ref[token].astype(jnp.float32)
        mixed = shared_ref[token]
        for k in range(2):
            output = outputs[slot_ref[k * count + token]].astype(jnp.float32)
            mixed = mixed + weight_ref[k * count + token] * output
            partial[k, token] = jnp.sum((cot * output).reshape(2, 8, LANES), axis=0)
        mixed_tiles[token] = mixed.astype(jnp.bfloat16)
        return carry

    def gather_grad(token, carry):
        grad = shared_grad_ref[token]
        for k in range(2):
            grad = grad + grads[slot_ref[k * count + token]].astype(jnp.float32)
        grad_tiles[token] = grad.astype(jnp.bfloat16)
        return carry

    copies[0].wait()
    lax.fori_loop(0, count, gather_output, 0, unroll=4)
    copies[1].wait()
    lax.fori_loop(0, count, gather_grad, 0, unroll=4)
    for group in range(count // TILE):
        at = slice(group * TILE, (group + 1) * TILE)
        both = jnp.concatenate(
            [mixed_tiles[at].reshape(256, LANES), grad_tiles[at].reshape(256, LANES)], axis=1
        )
        both = swap(perm, both)
        mixed_ref[at, :] = rows_from_stack(both[:, :LANES])
        grad_ref[at, :] = rows_from_stack(both[:, LANES:])
    ones = jnp.ones((8, LANES), jnp.float32)
    for k in range(2):
        sums = lax.dot_general(
            ones,
            jnp.sum(partial[k], axis=1),
            (((1,), (1,)), ((), ())),
            precision=lax.Precision.HIGHEST,
            preferred_element_type=jnp.float32,
        )
        gate_ref[k : k + 1, :] = sums[:1]


def combine(slots, weights, rows, cot, shared, shared_grad):
    count = cot.shape[0]
    width = TILE * LANES
    return pl.pallas_call(
        combine_kernel,
        out_shape=[
            jax.ShapeDtypeStruct((count, width), jnp.bfloat16),
            jax.ShapeDtypeStruct((count, width), jnp.bfloat16),
            jax.ShapeDtypeStruct((2, count), jnp.float32),
        ],
        in_specs=[pl.BlockSpec(memory_space=SMEM)] * 2
        + [pl.BlockSpec(memory_space=HBM)]
        + [pl.BlockSpec(memory_space=VMEM)] * 3,
        out_specs=[pl.BlockSpec(memory_space=VMEM)] * 3,
        scratch_shapes=[
            pltpu.VMEM((rows.shape[0], TILE, LANES), jnp.bfloat16),
            pltpu.VMEM((rows.shape[0], TILE, LANES), jnp.bfloat16),
            pltpu.VMEM((count, TILE, LANES), jnp.bfloat16),
            pltpu.VMEM((count, TILE, LANES), jnp.bfloat16),
            pltpu.VMEM((2, count, 8, LANES), jnp.float32),
            pltpu.SemaphoreType.DMA((2,)),
        ],
        compiler_params=pltpu.CompilerParams(vmem_limit_bytes=32 << 20),
        cost_estimate=pl.CostEstimate(
            flops=8 * 2 * 256**3, bytes_accessed=8 << 20, transcendentals=0
        ),
    )(slots, weights, rows, cot, shared, shared_grad)


def route_slots(chosen, count):
    number = jnp.arange(chosen.shape[0], dtype=jnp.int32)
    written = 2 * (number % count) + number // count
    same = (chosen[:, None] == chosen[None, :]) & (written[None, :] > written[:, None])
    return chosen * 2 + jnp.sum(same.astype(jnp.int32), axis=1)


def shared_expert(tokens, grad_out, gate, up, down, switch_vector):
    def dot(a, b, spec):
        return jnp.einsum(spec, a, b, preferred_element_type=jnp.float32)

    switch = jax.nn.sigmoid(jnp.dot(tokens, switch_vector, preferred_element_type=jnp.float32))
    pre_gate = dot(tokens, gate, "td,df->tf")
    pre_up = dot(tokens, up, "td,df->tf")
    hidden = (jax.nn.silu(pre_gate) * pre_up).astype(jnp.bfloat16)
    shared = dot(hidden, down, "tf,fd->td")
    cot = grad_out.astype(jnp.float32)
    shared_cot = (switch[:, None] * cot).astype(jnp.bfloat16)
    hidden_grad = dot(shared_cot, down, "td,fd->tf")
    gate_part = (hidden_grad * pre_up * silu_grad(pre_gate)).astype(jnp.bfloat16)
    up_part = (hidden_grad * jax.nn.silu(pre_gate)).astype(jnp.bfloat16)
    input_grad = dot(gate_part, gate, "tf,df->td") + dot(up_part, up, "tf,df->td")
    switch_grad = switch * (1.0 - switch) * jnp.sum(cot * shared, axis=1)
    grad = input_grad + switch_grad[:, None] * switch_vector.astype(jnp.float32)[None, :]
    return switch[:, None] * shared, grad


def local(
    tokens,
    expert_ids,
    gate_weights,
    grad_out,
    expert_gate,
    expert_up,
    expert_down,
    shared_gate,
    shared_up,
    shared_down,
    shared_switch,
):
    devices = lax.axis_size("tp") * lax.axis_size("ep")
    count = tokens.shape[0]
    tiled = (count, TILE, LANES)
    chosen = expert_ids.T.reshape(-1)
    weights = gate_weights.T.reshape(-1)
    sent = pack(chosen, weights, tokens, grad_out, devices)

    def exchange(rows):
        return lax.all_to_all(
            rows.reshape(devices, -1, LANES), AXES, split_axis=0, concat_axis=0, tiled=True
        ).reshape(2 * devices, 2, TILE, LANES)

    got = exchange(sent)
    all_in = lax.all_gather(
        jnp.concatenate([shared_gate, shared_up], axis=0), "tp", axis=1, tiled=True
    )
    got, all_in, shared_down, routes = lax.optimization_barrier((got, all_in, shared_down, chosen))
    all_gate, all_up = jnp.split(all_in, 2, axis=0)
    all_down = lax.all_gather(shared_down, "tp", axis=0, tiled=True)
    back = exchange(expert(got, expert_gate[0], expert_up[0], expert_down[0]))
    shared, shared_grad = shared_expert(
        tokens, grad_out, all_gate, all_up, all_down, shared_switch
    )
    mixed, grad_tokens, gate_grad = combine(
        route_slots(routes, count),
        weights,
        back,
        grad_out.reshape(tiled),
        shared.reshape(tiled),
        shared_grad.reshape(tiled),
    )
    return (mixed, grad_tokens, gate_grad.T)


def solution(mesh):
    rows = P(AXES, None)
    experts = P(AXES, None, None)
    placed = (rows, rows, rows, rows, experts, experts, experts)
    placed += (P(None, "tp"), P(None, "tp"), P("tp", None), P())
    return jax.shard_map(
        local, mesh=mesh, in_specs=placed, out_specs=(rows, rows, rows), check_vma=False
    )
```

```python
import jax
import jax.numpy as jnp
from jax import lax
from jax.experimental import pallas as pl
from jax.experimental.pallas import tpu as pltpu
from jax.sharding import PartitionSpec as P

AXES = ("tp", "ep")
LANES = 128
TILE = 16
VMEM = pltpu.VMEM
SMEM = pltpu.SMEM
HBM = pltpu.HBM
PARTS = 4


def silu_grad(argument):
    gate_sig = jax.nn.sigmoid(argument)
    return gate_sig * (1.0 + argument * (1.0 - gate_sig))


def swap_matrix():
    size = TILE * TILE
    row = lax.broadcasted_iota(jnp.int32, (size, size), 0)
    col = lax.broadcasted_iota(jnp.int32, (size, size), 1)
    return jnp.where(((row & 15) * 16 + (row >> 4)) == col, 1.0, 0.0).astype(jnp.bfloat16)


def swap(perm, block):
    return jnp.dot(perm, block, preferred_element_type=jnp.float32).astype(jnp.bfloat16)


def columns_stacked(block):
    return jnp.concatenate(
        [block[:, j * LANES : (j + 1) * LANES] for j in range(TILE)], axis=0
    )


def rows_from_stack(stack):
    return jnp.concatenate([stack[j * TILE : (j + 1) * TILE] for j in range(TILE)], axis=1)


def pack_kernel(
    chosen_ref, weight_ref, tokens_from, cot_from, out_ref, tokens, cots, token_tiles, cot_tiles,
    first, second, moved
):
    came = [
        pltpu.make_async_copy(tokens_from, tokens, moved.at[0]),
        pltpu.make_async_copy(cot_from, cots, moved.at[1]),
    ]
    for copy in came:
        copy.start()
    perm = swap_matrix()
    count = tokens.shape[0]
    zero = jnp.zeros((8, 2, TILE, LANES), jnp.bfloat16)

    def clear(step, carry):
        first[pl.ds(step * 8, 8)] = zero
        second[pl.ds(step * 8, 8)] = zero
        return carry

    lax.fori_loop(0, first.shape[0] // 8, clear, 0, unroll=4)
    for copy in came:
        copy.wait()
    for group in range(count // TILE):
        rows = slice(group * TILE, (group + 1) * TILE)
        both = jnp.concatenate(
            [columns_stacked(tokens[rows, :]), columns_stacked(cots[rows, :])], axis=1
        )
        both = swap(perm, both)
        token_tiles[rows] = both[:, :LANES].reshape(TILE, TILE, LANES)
        cot_tiles[rows] = both[:, LANES:].reshape(TILE, TILE, LANES)

    def place(slot, order, backward):
        def step(number, carry):
            token = count - 1 - number if backward else number
            row = token_tiles[token]
            cot = cot_tiles[token].astype(jnp.float32)
            for k in order:
                at = chosen_ref[k * count + token]
                slot[at, 0] = row
                slot[at, 1] = (weight_ref[k * count + token] * cot).astype(jnp.bfloat16)
            return carry

        lax.fori_loop(0, count, step, 0, unroll=4)

    gone = [
        pltpu.make_async_copy(first, out_ref.at[:, 0], moved.at[2]),
        pltpu.make_async_copy(second, out_ref.at[:, 1], moved.at[3]),
    ]
    place(first, (0, 1), False)
    gone[0].start()
    place(second, (1, 0), True)
    gone[1].start()
    for copy in gone:
        copy.wait()


def pack(chosen, weights, tokens, cot, experts):
    count = tokens.shape[0]
    return pl.pallas_call(
        pack_kernel,
        out_shape=jax.ShapeDtypeStruct((experts, 2, 2, TILE, LANES), jnp.bfloat16),
        in_specs=[pl.BlockSpec(memory_space=SMEM)] * 2 + [pl.BlockSpec(memory_space=HBM)] * 2,
        out_specs=pl.BlockSpec(memory_space=HBM),
        scratch_shapes=[pltpu.VMEM(tokens.shape, jnp.bfloat16)] * 2
        + [pltpu.VMEM((count, TILE, LANES), jnp.bfloat16)] * 2
        + [pltpu.VMEM((experts, 2, TILE, LANES), jnp.bfloat16)] * 2
        + [pltpu.SemaphoreType.DMA((4,))],
        compiler_params=pltpu.CompilerParams(vmem_limit_bytes=60 << 20),
        cost_estimate=pl.CostEstimate(
            flops=8 * 2 * 256**3, bytes_accessed=5 << 20, transcendentals=0
        ),
    )(chosen, weights, tokens, cot)


def expert_kernel(
    got_from, gate_from, up_from, down_from, back_to, got, back, rows, cots, outs, grads, gate_ref,
    up_ref, down_ref, arrived, came, gone
):
    perm = swap_matrix()
    blocks, count, width = rows.shape
    weights = [
        pltpu.make_async_copy(gate_from, gate_ref, arrived.at[0]),
        pltpu.make_async_copy(up_from, up_ref, arrived.at[1]),
        pltpu.make_async_copy(down_from, down_ref, arrived.at[2]),
    ]
    total = blocks * PARTS
    size = blocks * count // total
    groups = size // TILE

    def part(ref, number):
        return ref.at[pl.ds(number * size, size)]

    def load_copy(number):
        return pltpu.make_async_copy(part(got_from, number), part(got, number), came.at[number])

    def store_copy(number):
        return pltpu.make_async_copy(part(back, number), part(back_to, number), gone.at[number])

    for number in range(PARTS):
        load_copy(number).start()
    for copy in weights:
        copy.start()
    for number in range(PARTS, total):
        load_copy(number).start()
    one = (((1,), (0,)), ((), ()))
    other = (((1,), (1,)), ((), ()))

    def dot(a, b, dims):
        return lax.dot_general(a, b, dims, preferred_element_type=jnp.float32)

    for block in range(blocks):
        for number in range(block * PARTS, (block + 1) * PARTS):
            load_copy(number).wait()
            for group in range(groups):
                at = number * size + group * TILE
                tiles = got[at : at + TILE]
                both = jnp.concatenate(
                    [tiles[:, 0].reshape(256, LANES), tiles[:, 1].reshape(256, LANES)], axis=1
                )
                both = swap(perm, both)
                to = slice(at - block * count, at - block * count + TILE)
                rows[block, to, :] = rows_from_stack(both[:, :LANES])
                cots[block, to, :] = rows_from_stack(both[:, LANES:])
        if block == 0:
            weights[0].wait()
            weights[1].wait()
        pre_gate = dot(rows[block], gate_ref[...], one)
        pre_up = dot(rows[block], up_ref[...], one)
        sig = 1.0 / (1.0 + jnp.exp(-pre_gate))
        silu = pre_gate * sig
        hidden = (silu * pre_up).astype(jnp.bfloat16)
        if block == 0:
            weights[2].wait()
        outs[block] = dot(hidden, down_ref[...], one).astype(jnp.bfloat16)
        hidden_grad = dot(cots[block], down_ref[...], other)
        gate_part = hidden_grad * pre_up * (sig * (1.0 + pre_gate * (1.0 - sig)))
        gate_part = gate_part.astype(jnp.bfloat16)
        up_part = (hidden_grad * silu).astype(jnp.bfloat16)
        grads[block] = (
            dot(gate_part, gate_ref[...], other) + dot(up_part, up_ref[...], other)
        ).astype(jnp.bfloat16)
        for number in range(block * PARTS, (block + 1) * PARTS):
            for group in range(groups):
                at = number * size + group * TILE
                to = slice(at - block * count, at - block * count + TILE)
                both = jnp.concatenate(
                    [columns_stacked(outs[block, to, :]), columns_stacked(grads[block, to, :])],
                    axis=1,
                )
                both = swap(perm, both)
                back[at : at + TILE, 0] = both[:, :LANES].reshape(TILE, TILE, LANES)
                back[at : at + TILE, 1] = both[:, LANES:].reshape(TILE, TILE, LANES)
            store_copy(number).start()
    for number in range(total):
        store_copy(number).wait()


def expert(got, gate, up, down):
    blocks = 1
    count = got.shape[0] // blocks
    weights = [gate, up, down]
    return pl.pallas_call(
        expert_kernel,
        out_shape=jax.ShapeDtypeStruct(got.shape, jnp.bfloat16),
        in_specs=[pl.BlockSpec(memory_space=HBM)] * 4,
        out_specs=pl.BlockSpec(memory_space=HBM),
        scratch_shapes=[pltpu.VMEM(got.shape, jnp.bfloat16)] * 2
        + [pltpu.VMEM((blocks, count, gate.shape[0]), jnp.bfloat16)] * 4
        + [pltpu.VMEM(w.shape, jnp.bfloat16) for w in weights]
        + [pltpu.SemaphoreType.DMA((3,))]
        + [pltpu.SemaphoreType.DMA((blocks * PARTS,))] * 2,
        compiler_params=pltpu.CompilerParams(vmem_limit_bytes=50 << 20),
        cost_estimate=pl.CostEstimate(
            flops=512 * 2048 * 512 * 12, bytes_accessed=14 << 20, transcendentals=512 * 512
        ),
    )(got, *weights)


def combine_kernel(
    slot_ref, weight_ref, rows_from, cot_ref, shared_ref, shared_grad_ref, mixed_ref, grad_ref,
    gate_ref, outputs, grads, mixed_tiles, grad_tiles, partial, came
):
    copies = [
        pltpu.make_async_copy(rows_from.at[:, 0], outputs, came.at[0]),
        pltpu.make_async_copy(rows_from.at[:, 1], grads, came.at[1]),
    ]
    copies[0].start()
    perm = swap_matrix()
    count = cot_ref.shape[0]

    def gather_output(token, carry):
        cot = cot_ref[token].astype(jnp.float32)
        mixed = shared_ref[token]
        for k in range(2):
            output = outputs[slot_ref[k * count + token]].astype(jnp.float32)
            mixed = mixed + weight_ref[k * count + token] * output
            partial[k, token] = jnp.sum((cot * output).reshape(2, 8, LANES), axis=0)
        mixed_tiles[token] = mixed.astype(jnp.bfloat16)
        return carry

    def gather_grad(token, carry):
        grad = shared_grad_ref[token]
        for k in range(2):
            grad = grad + grads[slot_ref[k * count + token]].astype(jnp.float32)
        grad_tiles[token] = grad.astype(jnp.bfloat16)
        return carry

    copies[0].wait()
    copies[1].start()
    lax.fori_loop(0, count, gather_output, 0, unroll=16)
    copies[1].wait()
    lax.fori_loop(0, count, gather_grad, 0, unroll=16)
    for group in range(count // TILE):
        at = slice(group * TILE, (group + 1) * TILE)
        both = jnp.concatenate(
            [mixed_tiles[at].reshape(256, LANES), grad_tiles[at].reshape(256, LANES)], axis=1
        )
        both = swap(perm, both)
        mixed_ref[at, :] = rows_from_stack(both[:, :LANES])
        grad_ref[at, :] = rows_from_stack(both[:, LANES:])
    ones = jnp.ones((8, LANES), jnp.float32)
    for k in range(2):
        sums = lax.dot_general(
            ones,
            jnp.sum(partial[k], axis=1),
            (((1,), (1,)), ((), ())),
            precision=lax.Precision.HIGHEST,
            preferred_element_type=jnp.float32,
        )
        gate_ref[k : k + 1, :] = sums[:1]


def combine(slots, weights, rows, cot, shared, shared_grad):
    count = cot.shape[0]
    width = TILE * LANES
    return pl.pallas_call(
        combine_kernel,
        out_shape=[
            jax.ShapeDtypeStruct((count, width), jnp.bfloat16),
            jax.ShapeDtypeStruct((count, width), jnp.bfloat16),
            jax.ShapeDtypeStruct((2, count), jnp.float32),
        ],
        in_specs=[pl.BlockSpec(memory_space=SMEM)] * 2
        + [pl.BlockSpec(memory_space=HBM)]
        + [pl.BlockSpec(memory_space=VMEM)] * 3,
        out_specs=[pl.BlockSpec(memory_space=VMEM)] * 3,
        scratch_shapes=[
            pltpu.VMEM((rows.shape[0], TILE, LANES), jnp.bfloat16),
            pltpu.VMEM((rows.shape[0], TILE, LANES), jnp.bfloat16),
            pltpu.VMEM((count, TILE, LANES), jnp.bfloat16),
            pltpu.VMEM((count, TILE, LANES), jnp.bfloat16),
            pltpu.VMEM((2, count, 8, LANES), jnp.float32),
            pltpu.SemaphoreType.DMA((2,)),
        ],
        compiler_params=pltpu.CompilerParams(vmem_limit_bytes=32 << 20),
        cost_estimate=pl.CostEstimate(
            flops=8 * 2 * 256**3, bytes_accessed=8 << 20, transcendentals=0
        ),
    )(slots, weights, rows, cot, shared, shared_grad)


def route_slots(chosen, count):
    number = jnp.arange(chosen.shape[0], dtype=jnp.int32)
    written = 2 * (number % count) + number // count
    same = (chosen[:, None] == chosen[None, :]) & (written[None, :] > written[:, None])
    return chosen * 2 + jnp.sum(same.astype(jnp.int32), axis=1)


def shared_expert(tokens, grad_out, gate, up, down, switch_vector):
    def dot(a, b, spec):
        return jnp.einsum(spec, a, b, preferred_element_type=jnp.float32)

    switch = jax.nn.sigmoid(jnp.dot(tokens, switch_vector, preferred_element_type=jnp.float32))
    pre_gate = dot(tokens, gate, "td,df->tf")
    pre_up = dot(tokens, up, "td,df->tf")
    hidden = (jax.nn.silu(pre_gate) * pre_up).astype(jnp.bfloat16)
    shared = dot(hidden, down, "tf,fd->td")
    cot = grad_out.astype(jnp.float32)
    shared_cot = (switch[:, None] * cot).astype(jnp.bfloat16)
    hidden_grad = dot(shared_cot, down, "td,fd->tf")
    gate_part = (hidden_grad * pre_up * silu_grad(pre_gate)).astype(jnp.bfloat16)
    up_part = (hidden_grad * jax.nn.silu(pre_gate)).astype(jnp.bfloat16)
    input_grad = dot(gate_part, gate, "tf,df->td") + dot(up_part, up, "tf,df->td")
    switch_grad = switch * (1.0 - switch) * jnp.sum(cot * shared, axis=1)
    grad = input_grad + switch_grad[:, None] * switch_vector.astype(jnp.float32)[None, :]
    return switch[:, None] * shared, grad


def local(
    tokens,
    expert_ids,
    gate_weights,
    grad_out,
    expert_gate,
    expert_up,
    expert_down,
    shared_gate,
    shared_up,
    shared_down,
    shared_switch,
):
    devices = lax.axis_size("tp") * lax.axis_size("ep")
    count = tokens.shape[0]
    tiled = (count, TILE, LANES)
    chosen = expert_ids.T.reshape(-1)
    weights = gate_weights.T.reshape(-1)
    sent = pack(chosen, weights, tokens, grad_out, devices)

    def exchange(rows):
        return lax.all_to_all(
            rows.reshape(devices, -1, LANES), AXES, split_axis=0, concat_axis=0, tiled=True
        ).reshape(2 * devices, 2, TILE, LANES)

    got = exchange(sent)
    all_in = lax.all_gather(
        jnp.concatenate([shared_gate, shared_up], axis=0), "tp", axis=1, tiled=True
    )
    got, all_in, shared_down, routes = lax.optimization_barrier((got, all_in, shared_down, chosen))
    all_gate, all_up = jnp.split(all_in, 2, axis=0)
    all_down = lax.all_gather(shared_down, "tp", axis=0, tiled=True)
    back = exchange(expert(got, expert_gate[0], expert_up[0], expert_down[0]))
    shared, shared_grad = shared_expert(
        tokens, grad_out, all_gate, all_up, all_down, shared_switch
    )
    mixed, grad_tokens, gate_grad = combine(
        route_slots(routes, count),
        weights,
        back,
        grad_out.reshape(tiled),
        shared.reshape(tiled),
        shared_grad.reshape(tiled),
    )
    return (mixed, grad_tokens, gate_grad.T)


def solution(mesh):
    rows = P(AXES, None)
    experts = P(AXES, None, None)
    placed = (rows, rows, rows, rows, experts, experts, experts)
    placed += (P(None, "tp"), P(None, "tp"), P("tp", None), P())
    return jax.shard_map(
        local, mesh=mesh, in_specs=placed, out_specs=(rows, rows, rows), check_vma=False
    )
```

```python
import jax
import jax.numpy as jnp
from jax import lax
from jax.experimental import pallas as pl
from jax.experimental.pallas import tpu as pltpu
from jax.sharding import PartitionSpec as P

AXES = ("tp", "ep")
LANES = 128
TILE = 16
VMEM = pltpu.VMEM
SMEM = pltpu.SMEM
HBM = pltpu.HBM
PARTS = 4


def silu_grad(argument):
    gate_sig = jax.nn.sigmoid(argument)
    return gate_sig * (1.0 + argument * (1.0 - gate_sig))


def swap_matrix():
    size = TILE * TILE
    row = lax.broadcasted_iota(jnp.int32, (size, size), 0)
    col = lax.broadcasted_iota(jnp.int32, (size, size), 1)
    return jnp.where(((row & 15) * 16 + (row >> 4)) == col, 1.0, 0.0).astype(jnp.bfloat16)


def swap(perm, block):
    return jnp.dot(perm, block, preferred_element_type=jnp.float32).astype(jnp.bfloat16)


def columns_stacked(block):
    return jnp.concatenate(
        [block[:, j * LANES : (j + 1) * LANES] for j in range(TILE)], axis=0
    )


def rows_from_stack(stack):
    return jnp.concatenate([stack[j * TILE : (j + 1) * TILE] for j in range(TILE)], axis=1)


def pack_kernel(
    chosen_ref, weight_ref, tokens_from, cot_from, out_ref, tokens, cots, token_tiles, cot_tiles,
    first, second, moved
):
    came = [
        pltpu.make_async_copy(tokens_from, tokens, moved.at[0]),
        pltpu.make_async_copy(cot_from, cots, moved.at[1]),
    ]
    for copy in came:
        copy.start()
    perm = swap_matrix()
    count = tokens.shape[0]
    zero = jnp.zeros((8, 2, TILE, LANES), jnp.bfloat16)

    def clear(step, carry):
        first[pl.ds(step * 8, 8)] = zero
        second[pl.ds(step * 8, 8)] = zero
        return carry

    lax.fori_loop(0, first.shape[0] // 8, clear, 0, unroll=4)
    for copy in came:
        copy.wait()
    for group in range(count // TILE):
        rows = slice(group * TILE, (group + 1) * TILE)
        both = jnp.concatenate(
            [columns_stacked(tokens[rows, :]), columns_stacked(cots[rows, :])], axis=1
        )
        both = swap(perm, both)
        token_tiles[rows] = both[:, :LANES].reshape(TILE, TILE, LANES)
        cot_tiles[rows] = both[:, LANES:].reshape(TILE, TILE, LANES)

    def place(slot, order, backward):
        def step(number, carry):
            token = count - 1 - number if backward else number
            row = token_tiles[token]
            cot = cot_tiles[token].astype(jnp.float32)
            for k in order:
                at = chosen_ref[k * count + token]
                slot[at, 0] = row
                slot[at, 1] = (weight_ref[k * count + token] * cot).astype(jnp.bfloat16)
            return carry

        lax.fori_loop(0, count, step, 0, unroll=4)

    gone = [
        pltpu.make_async_copy(first, out_ref.at[:, 0], moved.at[2]),
        pltpu.make_async_copy(second, out_ref.at[:, 1], moved.at[3]),
    ]
    place(first, (0, 1), False)
    gone[0].start()
    place(second, (1, 0), True)
    gone[1].start()
    for copy in gone:
        copy.wait()


def pack(chosen, weights, tokens, cot, experts):
    count = tokens.shape[0]
    return pl.pallas_call(
        pack_kernel,
        out_shape=jax.ShapeDtypeStruct((experts, 2, 2, TILE, LANES), jnp.bfloat16),
        in_specs=[pl.BlockSpec(memory_space=SMEM)] * 2 + [pl.BlockSpec(memory_space=HBM)] * 2,
        out_specs=pl.BlockSpec(memory_space=HBM),
        scratch_shapes=[pltpu.VMEM(tokens.shape, jnp.bfloat16)] * 2
        + [pltpu.VMEM((count, TILE, LANES), jnp.bfloat16)] * 2
        + [pltpu.VMEM((experts, 2, TILE, LANES), jnp.bfloat16)] * 2
        + [pltpu.SemaphoreType.DMA((4,))],
        compiler_params=pltpu.CompilerParams(vmem_limit_bytes=60 << 20),
        cost_estimate=pl.CostEstimate(
            flops=8 * 2 * 256**3, bytes_accessed=5 << 20, transcendentals=0
        ),
    )(chosen, weights, tokens, cot)


def expert_kernel(
    got_from, gate_from, up_from, down_from, back_to, got, back, rows, cots, outs, grads, gate_ref,
    up_ref, down_ref, arrived, came, gone
):
    perm = swap_matrix()
    blocks, count, width = rows.shape
    weights = [
        pltpu.make_async_copy(gate_from, gate_ref, arrived.at[0]),
        pltpu.make_async_copy(up_from, up_ref, arrived.at[1]),
        pltpu.make_async_copy(down_from, down_ref, arrived.at[2]),
    ]
    total = blocks * PARTS
    size = blocks * count // total
    groups = size // TILE

    def part(ref, number):
        return ref.at[pl.ds(number * size, size)]

    def load_copy(number):
        return pltpu.make_async_copy(part(got_from, number), part(got, number), came.at[number])

    def store_copy(number):
        return pltpu.make_async_copy(part(back, number), part(back_to, number), gone.at[number])

    for number in range(PARTS):
        load_copy(number).start()
    for copy in weights:
        copy.start()
    for number in range(PARTS, total):
        load_copy(number).start()
    one = (((1,), (0,)), ((), ()))
    other = (((1,), (1,)), ((), ()))

    def dot(a, b, dims):
        return lax.dot_general(a, b, dims, preferred_element_type=jnp.float32)

    for block in range(blocks):
        for number in range(block * PARTS, (block + 1) * PARTS):
            load_copy(number).wait()
            for group in range(groups):
                at = number * size + group * TILE
                tiles = got[at : at + TILE]
                both = jnp.concatenate(
                    [tiles[:, 0].reshape(256, LANES), tiles[:, 1].reshape(256, LANES)], axis=1
                )
                both = swap(perm, both)
                to = slice(at - block * count, at - block * count + TILE)
                rows[block, to, :] = rows_from_stack(both[:, :LANES])
                cots[block, to, :] = rows_from_stack(both[:, LANES:])
        if block == 0:
            weights[0].wait()
            weights[1].wait()
        pre_gate = dot(rows[block], gate_ref[...], one)
        pre_up = dot(rows[block], up_ref[...], one)
        sig = 1.0 / (1.0 + jnp.exp(-pre_gate))
        silu = pre_gate * sig
        hidden = (silu * pre_up).astype(jnp.bfloat16)
        if block == 0:
            weights[2].wait()
        outs[block] = dot(hidden, down_ref[...], one).astype(jnp.bfloat16)
        hidden_grad = dot(cots[block], down_ref[...], other)
        gate_part = hidden_grad * pre_up * (sig * (1.0 + pre_gate * (1.0 - sig)))
        gate_part = gate_part.astype(jnp.bfloat16)
        up_part = (hidden_grad * silu).astype(jnp.bfloat16)
        grads[block] = (
            dot(gate_part, gate_ref[...], other) + dot(up_part, up_ref[...], other)
        ).astype(jnp.bfloat16)
        for number in range(block * PARTS, (block + 1) * PARTS):
            for group in range(groups):
                at = number * size + group * TILE
                to = slice(at - block * count, at - block * count + TILE)
                both = jnp.concatenate(
                    [columns_stacked(outs[block, to, :]), columns_stacked(grads[block, to, :])],
                    axis=1,
                )
                both = swap(perm, both)
                back[at : at + TILE, 0] = both[:, :LANES].reshape(TILE, TILE, LANES)
                back[at : at + TILE, 1] = both[:, LANES:].reshape(TILE, TILE, LANES)
            store_copy(number).start()
    for number in range(total):
        store_copy(number).wait()


def expert(got, gate, up, down):
    blocks = 1
    count = got.shape[0] // blocks
    weights = [gate, up, down]
    return pl.pallas_call(
        expert_kernel,
        out_shape=jax.ShapeDtypeStruct(got.shape, jnp.bfloat16),
        in_specs=[pl.BlockSpec(memory_space=HBM)] * 4,
        out_specs=pl.BlockSpec(memory_space=HBM),
        scratch_shapes=[pltpu.VMEM(got.shape, jnp.bfloat16)] * 2
        + [pltpu.VMEM((blocks, count, gate.shape[0]), jnp.bfloat16)] * 4
        + [pltpu.VMEM(w.shape, jnp.bfloat16) for w in weights]
        + [pltpu.SemaphoreType.DMA((3,))]
        + [pltpu.SemaphoreType.DMA((blocks * PARTS,))] * 2,
        compiler_params=pltpu.CompilerParams(vmem_limit_bytes=50 << 20),
        cost_estimate=pl.CostEstimate(
            flops=512 * 2048 * 512 * 12, bytes_accessed=14 << 20, transcendentals=512 * 512
        ),
    )(got, *weights)


def combine_kernel(
    slot_ref, weight_ref, rows_from, cot_ref, shared_ref, shared_grad_ref, mixed_ref, grad_ref,
    gate_ref, outputs, grads, mixed_tiles, grad_tiles, partial, came
):
    copies = [
        pltpu.make_async_copy(rows_from.at[:, 0], outputs, came.at[0]),
        pltpu.make_async_copy(rows_from.at[:, 1], grads, came.at[1]),
    ]
    for copy in copies:
        copy.start()
    perm = swap_matrix()
    count = cot_ref.shape[0]

    def gather_output(token, carry):
        cot = cot_ref[token].astype(jnp.float32)
        mixed = shared_ref[token]
        for k in range(2):
            output = outputs[slot_ref[k * count + token]].astype(jnp.float32)
            mixed = mixed + weight_ref[k * count + token] * output
            partial[k, token] = jnp.sum((cot * output).reshape(2, 8, LANES), axis=0)
        mixed_tiles[token] = mixed.astype(jnp.bfloat16)
        return carry

    def gather_grad(token, carry):
        grad = shared_grad_ref[token]
        for k in range(2):
            grad = grad + grads[slot_ref[k * count + token]].astype(jnp.float32)
        grad_tiles[token] = grad.astype(jnp.bfloat16)
        return carry

    copies[0].wait()
    lax.fori_loop(0, count, gather_output, 0, unroll=4)
    copies[1].wait()
    lax.fori_loop(0, count, gather_grad, 0, unroll=4)
    for group in range(count // TILE):
        at = slice(group * TILE, (group + 1) * TILE)
        both = jnp.concatenate(
            [mixed_tiles[at].reshape(256, LANES), grad_tiles[at].reshape(256, LANES)], axis=1
        )
        both = swap(perm, both)
        mixed_ref[at, :] = rows_from_stack(both[:, :LANES])
        grad_ref[at, :] = rows_from_stack(both[:, LANES:])
    ones = jnp.ones((8, LANES), jnp.float32)
    for k in range(2):
        sums = lax.dot_general(
            ones,
            jnp.sum(partial[k], axis=1),
            (((1,), (1,)), ((), ())),
            precision=lax.Precision.HIGHEST,
            preferred_element_type=jnp.float32,
        )
        gate_ref[k : k + 1, :] = sums[:1]


def combine(slots, weights, rows, cot, shared, shared_grad):
    count = cot.shape[0]
    width = TILE * LANES
    return pl.pallas_call(
        combine_kernel,
        out_shape=[
            jax.ShapeDtypeStruct((count, width), jnp.bfloat16),
            jax.ShapeDtypeStruct((count, width), jnp.bfloat16),
            jax.ShapeDtypeStruct((2, count), jnp.float32),
        ],
        in_specs=[pl.BlockSpec(memory_space=SMEM)] * 2
        + [pl.BlockSpec(memory_space=HBM)]
        + [pl.BlockSpec(memory_space=VMEM)] * 3,
        out_specs=[pl.BlockSpec(memory_space=VMEM)] * 3,
        scratch_shapes=[
            pltpu.VMEM((rows.shape[0], TILE, LANES), jnp.bfloat16),
            pltpu.VMEM((rows.shape[0], TILE, LANES), jnp.bfloat16),
            pltpu.VMEM((count, TILE, LANES), jnp.bfloat16),
            pltpu.VMEM((count, TILE, LANES), jnp.bfloat16),
            pltpu.VMEM((2, count, 8, LANES), jnp.float32),
            pltpu.SemaphoreType.DMA((2,)),
        ],
        compiler_params=pltpu.CompilerParams(vmem_limit_bytes=32 << 20),
        cost_estimate=pl.CostEstimate(
            flops=8 * 2 * 256**3, bytes_accessed=8 << 20, transcendentals=0
        ),
    )(slots, weights, rows, cot, shared, shared_grad)


def route_slots(chosen, count):
    number = jnp.arange(chosen.shape[0], dtype=jnp.int32)
    written = 2 * (number % count) + number // count
    same = (chosen[:, None] == chosen[None, :]) & (written[None, :] > written[:, None])
    return chosen * 2 + jnp.sum(same.astype(jnp.int32), axis=1)


def shared_expert(tokens, grad_out, gate, up, down, switch_vector):
    def dot(a, b, spec):
        return jnp.einsum(spec, a, b, preferred_element_type=jnp.float32)

    switch = jax.nn.sigmoid(jnp.dot(tokens, switch_vector, preferred_element_type=jnp.float32))
    pre_gate = dot(tokens, gate, "td,df->tf")
    pre_up = dot(tokens, up, "td,df->tf")
    hidden = (jax.nn.silu(pre_gate) * pre_up).astype(jnp.bfloat16)
    shared = dot(hidden, down, "tf,fd->td")
    cot = grad_out.astype(jnp.float32)
    shared_cot = (switch[:, None] * cot).astype(jnp.bfloat16)
    hidden_grad = dot(shared_cot, down, "td,fd->tf")
    gate_part = (hidden_grad * pre_up * silu_grad(pre_gate)).astype(jnp.bfloat16)
    up_part = (hidden_grad * jax.nn.silu(pre_gate)).astype(jnp.bfloat16)
    input_grad = dot(gate_part, gate, "tf,df->td") + dot(up_part, up, "tf,df->td")
    switch_grad = switch * (1.0 - switch) * jnp.sum(cot * shared, axis=1)
    grad = input_grad + switch_grad[:, None] * switch_vector.astype(jnp.float32)[None, :]
    return switch[:, None] * shared, grad


def local(
    tokens,
    expert_ids,
    gate_weights,
    grad_out,
    expert_gate,
    expert_up,
    expert_down,
    shared_gate,
    shared_up,
    shared_down,
    shared_switch,
):
    devices = lax.axis_size("tp") * lax.axis_size("ep")
    count = tokens.shape[0]
    tiled = (count, TILE, LANES)
    chosen = expert_ids.T.reshape(-1)
    weights = gate_weights.T.reshape(-1)
    sent = pack(chosen, weights, tokens, grad_out, devices)

    def exchange(rows):
        return lax.all_to_all(
            rows.reshape(devices, -1, LANES), AXES, split_axis=0, concat_axis=0, tiled=True
        ).reshape(2 * devices, 2, TILE, LANES)

    got = exchange(sent)
    all_in = lax.all_gather(
        jnp.concatenate([shared_gate, shared_up], axis=0), "tp", axis=1, tiled=True
    )
    got, all_in, shared_down, routes = lax.optimization_barrier((got, all_in, shared_down, chosen))
    all_gate, all_up = jnp.split(all_in, 2, axis=0)
    all_down = lax.all_gather(shared_down, "tp", axis=0, tiled=True)
    back = exchange(expert(got, expert_gate[0], expert_up[0], expert_down[0]))
    shared, shared_grad = shared_expert(
        tokens, grad_out, all_gate, all_up, all_down, shared_switch
    )
    mixed, grad_tokens, gate_grad = combine(
        route_slots(routes, count),
        weights,
        back,
        grad_out.reshape(tiled),
        shared.reshape(tiled),
        shared_grad.reshape(tiled),
    )
    return (mixed, grad_tokens, gate_grad.T)


def solution(mesh):
    rows = P(AXES, None)
    experts = P(AXES, None, None)
    placed = (rows, rows, rows, rows, experts, experts, experts)
    placed += (P(None, "tp"), P(None, "tp"), P("tp", None), P())
    return jax.shard_map(
        local, mesh=mesh, in_specs=placed, out_specs=(rows, rows, rows), check_vma=False
    )
```

```python
import jax
import jax.numpy as jnp
from jax import lax
from jax.experimental import pallas as pl
from jax.experimental.pallas import tpu as pltpu
from jax.sharding import PartitionSpec as P

AXES = ("tp", "ep")
LANES = 128
TILE = 16
VMEM = pltpu.VMEM
SMEM = pltpu.SMEM
HBM = pltpu.HBM
PARTS = 4


def silu_grad(argument):
    gate_sig = jax.nn.sigmoid(argument)
    return gate_sig * (1.0 + argument * (1.0 - gate_sig))


def swap_matrix():
    size = TILE * TILE
    row = lax.broadcasted_iota(jnp.int32, (size, size), 0)
    col = lax.broadcasted_iota(jnp.int32, (size, size), 1)
    return jnp.where(((row & 15) * 16 + (row >> 4)) == col, 1.0, 0.0).astype(jnp.bfloat16)


def swap(perm, block):
    return jnp.dot(perm, block, preferred_element_type=jnp.float32).astype(jnp.bfloat16)


def columns_stacked(block):
    return jnp.concatenate(
        [block[:, j * LANES : (j + 1) * LANES] for j in range(TILE)], axis=0
    )


def rows_from_stack(stack):
    return jnp.concatenate([stack[j * TILE : (j + 1) * TILE] for j in range(TILE)], axis=1)


def pack_kernel(
    chosen_ref, weight_ref, tokens_from, cot_from, out_ref, tokens, cots, token_tiles, cot_tiles,
    first, second, moved
):
    came = [
        pltpu.make_async_copy(tokens_from, tokens, moved.at[0]),
        pltpu.make_async_copy(cot_from, cots, moved.at[1]),
    ]
    for copy in came:
        copy.start()
    perm = swap_matrix()
    count = tokens.shape[0]
    zero = jnp.zeros((8, 2, TILE, LANES), jnp.bfloat16)

    def clear(step, carry):
        first[pl.ds(step * 8, 8)] = zero
        second[pl.ds(step * 8, 8)] = zero
        return carry

    lax.fori_loop(0, first.shape[0] // 8, clear, 0, unroll=4)
    for copy in came:
        copy.wait()
    for group in range(count // TILE):
        rows = slice(group * TILE, (group + 1) * TILE)
        both = jnp.concatenate(
            [columns_stacked(tokens[rows, :]), columns_stacked(cots[rows, :])], axis=1
        )
        both = swap(perm, both)
        token_tiles[rows] = both[:, :LANES].reshape(TILE, TILE, LANES)
        cot_tiles[rows] = both[:, LANES:].reshape(TILE, TILE, LANES)

    def place(slot, order, backward):
        def step(number, carry):
            token = count - 1 - number if backward else number
            row = token_tiles[token]
            cot = cot_tiles[token].astype(jnp.float32)
            for k in order:
                at = chosen_ref[k * count + token]
                slot[at, 0] = row
                slot[at, 1] = (weight_ref[k * count + token] * cot).astype(jnp.bfloat16)
            return carry

        lax.fori_loop(0, count, step, 0, unroll=4)

    gone = [
        pltpu.make_async_copy(first, out_ref.at[:, 0], moved.at[2]),
        pltpu.make_async_copy(second, out_ref.at[:, 1], moved.at[3]),
    ]
    place(first, (0, 1), False)
    gone[0].start()
    place(second, (1, 0), True)
    gone[1].start()
    for copy in gone:
        copy.wait()


def pack(chosen, weights, tokens, cot, experts):
    count = tokens.shape[0]
    return pl.pallas_call(
        pack_kernel,
        out_shape=jax.ShapeDtypeStruct((experts, 2, 2, TILE, LANES), jnp.bfloat16),
        in_specs=[pl.BlockSpec(memory_space=SMEM)] * 2 + [pl.BlockSpec(memory_space=HBM)] * 2,
        out_specs=pl.BlockSpec(memory_space=HBM),
        scratch_shapes=[pltpu.VMEM(tokens.shape, jnp.bfloat16)] * 2
        + [pltpu.VMEM((count, TILE, LANES), jnp.bfloat16)] * 2
        + [pltpu.VMEM((experts, 2, TILE, LANES), jnp.bfloat16)] * 2
        + [pltpu.SemaphoreType.DMA((4,))],
        compiler_params=pltpu.CompilerParams(vmem_limit_bytes=60 << 20),
        cost_estimate=pl.CostEstimate(
            flops=8 * 2 * 256**3, bytes_accessed=5 << 20, transcendentals=0
        ),
    )(chosen, weights, tokens, cot)


def expert_kernel(
    got_from, gate_from, up_from, down_from, back_to, got, back, rows, cots, outs, grads, gate_ref,
    up_ref, down_ref, arrived, came, gone
):
    perm = swap_matrix()
    blocks, count, width = rows.shape
    weights = [
        pltpu.make_async_copy(gate_from, gate_ref, arrived.at[0]),
        pltpu.make_async_copy(up_from, up_ref, arrived.at[1]),
        pltpu.make_async_copy(down_from, down_ref, arrived.at[2]),
    ]
    total = blocks * PARTS
    size = blocks * count // total
    groups = size // TILE

    def part(ref, number):
        return ref.at[pl.ds(number * size, size)]

    def load_copy(number):
        return pltpu.make_async_copy(part(got_from, number), part(got, number), came.at[number])

    def store_copy(number):
        return pltpu.make_async_copy(part(back, number), part(back_to, number), gone.at[number])

    for number in range(PARTS):
        load_copy(number).start()
    for copy in weights:
        copy.start()
    for number in range(PARTS, total):
        load_copy(number).start()
    one = (((1,), (0,)), ((), ()))
    other = (((1,), (1,)), ((), ()))

    def dot(a, b, dims):
        return lax.dot_general(a, b, dims, preferred_element_type=jnp.float32)

    for block in range(blocks):
        for number in range(block * PARTS, (block + 1) * PARTS):
            load_copy(number).wait()
            for group in range(groups):
                at = number * size + group * TILE
                tiles = got[at : at + TILE]
                both = jnp.concatenate(
                    [tiles[:, 0].reshape(256, LANES), tiles[:, 1].reshape(256, LANES)], axis=1
                )
                both = swap(perm, both)
                to = slice(at - block * count, at - block * count + TILE)
                rows[block, to, :] = rows_from_stack(both[:, :LANES])
                cots[block, to, :] = rows_from_stack(both[:, LANES:])
        if block == 0:
            weights[0].wait()
            weights[1].wait()
        pre_gate = dot(rows[block], gate_ref[...], one)
        pre_up = dot(rows[block], up_ref[...], one)
        sig = 1.0 / (1.0 + jnp.exp(-pre_gate))
        silu = pre_gate * sig
        hidden = (silu * pre_up).astype(jnp.bfloat16)
        if block == 0:
            weights[2].wait()
        outs[block] = dot(hidden, down_ref[...], one).astype(jnp.bfloat16)
        hidden_grad = dot(cots[block], down_ref[...], other)
        gate_part = hidden_grad * pre_up * (sig * (1.0 + pre_gate * (1.0 - sig)))
        gate_part = gate_part.astype(jnp.bfloat16)
        up_part = (hidden_grad * silu).astype(jnp.bfloat16)
        grads[block] = (
            dot(gate_part, gate_ref[...], other) + dot(up_part, up_ref[...], other)
        ).astype(jnp.bfloat16)
        for number in range(block * PARTS, (block + 1) * PARTS):
            for group in range(groups):
                at = number * size + group * TILE
                to = slice(at - block * count, at - block * count + TILE)
                both = jnp.concatenate(
                    [columns_stacked(outs[block, to, :]), columns_stacked(grads[block, to, :])],
                    axis=1,
                )
                both = swap(perm, both)
                back[at : at + TILE, 0] = both[:, :LANES].reshape(TILE, TILE, LANES)
                back[at : at + TILE, 1] = both[:, LANES:].reshape(TILE, TILE, LANES)
            store_copy(number).start()
    for number in range(total):
        store_copy(number).wait()


def expert(got, gate, up, down):
    blocks = 1
    count = got.shape[0] // blocks
    weights = [gate, up, down]
    return pl.pallas_call(
        expert_kernel,
        out_shape=jax.ShapeDtypeStruct(got.shape, jnp.bfloat16),
        in_specs=[pl.BlockSpec(memory_space=HBM)] * 4,
        out_specs=pl.BlockSpec(memory_space=HBM),
        scratch_shapes=[pltpu.VMEM(got.shape, jnp.bfloat16)] * 2
        + [pltpu.VMEM((blocks, count, gate.shape[0]), jnp.bfloat16)] * 4
        + [pltpu.VMEM(w.shape, jnp.bfloat16) for w in weights]
        + [pltpu.SemaphoreType.DMA((3,))]
        + [pltpu.SemaphoreType.DMA((blocks * PARTS,))] * 2,
        compiler_params=pltpu.CompilerParams(vmem_limit_bytes=50 << 20),
        cost_estimate=pl.CostEstimate(
            flops=512 * 2048 * 512 * 12, bytes_accessed=14 << 20, transcendentals=512 * 512
        ),
    )(got, *weights)


def combine_kernel(
    slot_ref, weight_ref, rows_from, cot_ref, shared_ref, shared_grad_ref, mixed_ref, grad_ref,
    gate_ref, tiles, mixed_tiles, grad_tiles, partial, came
):
    size = tiles.shape[0] // PARTS
    copies = [
        pltpu.make_async_copy(
            rows_from.at[pl.ds(part * size, size)],
            tiles.at[pl.ds(part * size, size)],
            came.at[part],
        )
        for part in range(PARTS)
    ]
    for copy in copies:
        copy.start()
    perm = swap_matrix()
    count = cot_ref.shape[0]

    def gather(token, carry):
        cot = cot_ref[token].astype(jnp.float32)
        mixed = shared_ref[token]
        grad = shared_grad_ref[token]
        for k in range(2):
            at = slot_ref[k * count + token]
            output = tiles[at, 0].astype(jnp.float32)
            mixed = mixed + weight_ref[k * count + token] * output
            grad = grad + tiles[at, 1].astype(jnp.float32)
            partial[k, token] = jnp.sum((cot * output).reshape(2, 8, LANES), axis=0)
        mixed_tiles[token] = mixed.astype(jnp.bfloat16)
        grad_tiles[token] = grad.astype(jnp.bfloat16)
        return carry

    for copy in copies:
        copy.wait()
    lax.fori_loop(0, count, gather, 0, unroll=4)
    for group in range(count // TILE):
        at = slice(group * TILE, (group + 1) * TILE)
        both = jnp.concatenate(
            [mixed_tiles[at].reshape(256, LANES), grad_tiles[at].reshape(256, LANES)], axis=1
        )
        both = swap(perm, both)
        mixed_ref[at, :] = rows_from_stack(both[:, :LANES])
        grad_ref[at, :] = rows_from_stack(both[:, LANES:])
    ones = jnp.ones((8, LANES), jnp.float32)
    for k in range(2):
        sums = lax.dot_general(
            ones,
            jnp.sum(partial[k], axis=1),
            (((1,), (1,)), ((), ())),
            precision=lax.Precision.HIGHEST,
            preferred_element_type=jnp.float32,
        )
        gate_ref[k : k + 1, :] = sums[:1]


def combine(slots, weights, rows, cot, shared, shared_grad):
    count = cot.shape[0]
    width = TILE * LANES
    return pl.pallas_call(
        combine_kernel,
        out_shape=[
            jax.ShapeDtypeStruct((count, width), jnp.bfloat16),
            jax.ShapeDtypeStruct((count, width), jnp.bfloat16),
            jax.ShapeDtypeStruct((2, count), jnp.float32),
        ],
        in_specs=[pl.BlockSpec(memory_space=SMEM)] * 2
        + [pl.BlockSpec(memory_space=HBM)]
        + [pl.BlockSpec(memory_space=VMEM)] * 3,
        out_specs=[pl.BlockSpec(memory_space=VMEM)] * 3,
        scratch_shapes=[
            pltpu.VMEM(rows.shape, jnp.bfloat16),
            pltpu.VMEM((count, TILE, LANES), jnp.bfloat16),
            pltpu.VMEM((count, TILE, LANES), jnp.bfloat16),
            pltpu.VMEM((2, count, 8, LANES), jnp.float32),
            pltpu.SemaphoreType.DMA((PARTS,)),
        ],
        compiler_params=pltpu.CompilerParams(vmem_limit_bytes=32 << 20),
        cost_estimate=pl.CostEstimate(
            flops=8 * 2 * 256**3, bytes_accessed=8 << 20, transcendentals=0
        ),
    )(slots, weights, rows, cot, shared, shared_grad)


def route_slots(chosen, count):
    number = jnp.arange(chosen.shape[0], dtype=jnp.int32)
    written = 2 * (number % count) + number // count
    same = (chosen[:, None] == chosen[None, :]) & (written[None, :] > written[:, None])
    return chosen * 2 + jnp.sum(same.astype(jnp.int32), axis=1)


def shared_expert(tokens, grad_out, gate, up, down, switch_vector):
    def dot(a, b, spec):
        return jnp.einsum(spec, a, b, preferred_element_type=jnp.float32)

    switch = jax.nn.sigmoid(jnp.dot(tokens, switch_vector, preferred_element_type=jnp.float32))
    pre_gate = dot(tokens, gate, "td,df->tf")
    pre_up = dot(tokens, up, "td,df->tf")
    hidden = (jax.nn.silu(pre_gate) * pre_up).astype(jnp.bfloat16)
    shared = dot(hidden, down, "tf,fd->td")
    cot = grad_out.astype(jnp.float32)
    shared_cot = (switch[:, None] * cot).astype(jnp.bfloat16)
    hidden_grad = dot(shared_cot, down, "td,fd->tf")
    gate_part = (hidden_grad * pre_up * silu_grad(pre_gate)).astype(jnp.bfloat16)
    up_part = (hidden_grad * jax.nn.silu(pre_gate)).astype(jnp.bfloat16)
    input_grad = dot(gate_part, gate, "tf,df->td") + dot(up_part, up, "tf,df->td")
    switch_grad = switch * (1.0 - switch) * jnp.sum(cot * shared, axis=1)
    grad = input_grad + switch_grad[:, None] * switch_vector.astype(jnp.float32)[None, :]
    return switch[:, None] * shared, grad


def local(
    tokens,
    expert_ids,
    gate_weights,
    grad_out,
    expert_gate,
    expert_up,
    expert_down,
    shared_gate,
    shared_up,
    shared_down,
    shared_switch,
):
    devices = lax.axis_size("tp") * lax.axis_size("ep")
    count = tokens.shape[0]
    tiled = (count, TILE, LANES)
    chosen = expert_ids.T.reshape(-1)
    weights = gate_weights.T.reshape(-1)
    sent = pack(chosen, weights, tokens, grad_out, devices)

    def exchange(rows):
        return lax.all_to_all(
            rows.reshape(devices, -1, LANES), AXES, split_axis=0, concat_axis=0, tiled=True
        ).reshape(2 * devices, 2, TILE, LANES)

    got = exchange(sent)
    all_in = lax.all_gather(
        jnp.concatenate([shared_gate, shared_up], axis=0), "tp", axis=1, tiled=True
    )
    got, all_in, shared_down, routes = lax.optimization_barrier((got, all_in, shared_down, chosen))
    all_gate, all_up = jnp.split(all_in, 2, axis=0)
    all_down = lax.all_gather(shared_down, "tp", axis=0, tiled=True)
    back = exchange(expert(got, expert_gate[0], expert_up[0], expert_down[0]))
    shared, shared_grad = shared_expert(
        tokens, grad_out, all_gate, all_up, all_down, shared_switch
    )
    mixed, grad_tokens, gate_grad = combine(
        route_slots(routes, count),
        weights,
        back,
        grad_out.reshape(tiled),
        shared.reshape(tiled),
        shared_grad.reshape(tiled),
    )
    return (mixed, grad_tokens, gate_grad.T)


def solution(mesh):
    rows = P(AXES, None)
    experts = P(AXES, None, None)
    placed = (rows, rows, rows, rows, experts, experts, experts)
    placed += (P(None, "tp"), P(None, "tp"), P("tp", None), P())
    return jax.shard_map(
        local, mesh=mesh, in_specs=placed, out_specs=(rows, rows, rows), check_vma=False
    )
```
